32 devices in a mesh: grp: 2 (over y), blk: 8 (over z, x), pair: 2 (over core).
Axes of the slice: x: 2, y: 2, z: 4, core: 2. Of those that a mesh axis runs over, the one named last changes fastest.
Arguments:
- wavefunc: bfloat16 [96, 16, 2, 768], P(('grp', 'blk')), parts along dimension 0, may hold values from -6 to 6
- haydock: float32 [96, 128], P(('grp', 'blk')), parts along dimension 0, may hold values from -6 to 6
- screened: bfloat16 [16, 768, 768], P(('grp', 'blk')), parts along dimension 0, may hold values from -0.21875 to 0.21875
- coulomb: float32 [1536], P('grp'), parts along dimension 0, may hold values from 0.05 to 1
- umklapp_map: int32 [3, 768], replicated, may hold values from 0 to 767, each once within a row
Outputs:
- kernel_out: float32 [96, 128], P(('grp', 'blk')), parts along dimension 0
The draws below stay inside these ranges and needn't reach their ends.
There are 2 independent parts, one for each index of `grp`. The reference program is written for one: setup_inputs(seed, part) draws one part's arguments, and reference() takes and returns one part's arrays. A program takes and returns all parts, laid end to end along the dimension named above; an argument that names none is the same for every part. Nothing has to cross between parts.
Inputs may be any that keep to these rules, and one draw needn't show every extreme that they name: Each row of umklapp_map is a permutation of 0 .. 767.
All inputs are finite; a program needn't handle non-finite values.
Results may differ from the reference program's by a relative error of at most 0.015.
Values may be sent and summed in bfloat16 or wider, within the bound.
No kernel may reach another device: no remote copies, remote signals or barrier semaphores. Data moves between devices by JAX's collectives and lax.ppermute only.
A program may use at most 64 MiB of HBM per device.

```python
import math
import jax
import jax.numpy as jnp
from jax import lax

NV = 8
NC = 8
NG = 768
KR = 6
STOPS = 2
NB = 16
QS = 8
NK = 48
NPSI = 128


def levels(key, extent, cuts, low, largest):
    factor_of, own = 1.0, jax.random.fold_in(key, 6)
    for dim, parts in cuts:
        heights = jnp.exp(jax.random.uniform(jax.random.fold_in(own, dim), (parts,), jnp.float32, low / len(cuts), largest / len(cuts)))
        factor_of = factor_of * jnp.repeat(heights, extent[dim] // parts).reshape([-1 if axis == dim else 1 for axis in range(len(extent))])
    return factor_of


def noise(own_key, dims, spread, limit, pieces=(), kind=jnp.bfloat16):
    factor_of = levels(own_key, dims, pieces, -0.22, 0.18) if pieces else 1.0
    drawn = jax.random.normal(own_key, dims, jnp.float32) * spread * factor_of
    return jnp.minimum(jnp.maximum(drawn, -limit), limit).astype(kind)


def setup_inputs(seed: int = 0, part: int = 0) -> dict:
    keys = jax.random.split(jax.random.key(seed), 6)
    own_keys = jax.random.split(jax.random.fold_in(keys[5], part), 6)
    return {
        "wavefunc": noise(own_keys[0], (NK, NB, 2, NG), 1.0, 6.0, ((0, 8),)),
        "haydock": noise(own_keys[1], (NK, NPSI), 1.0, 6.0, ((0, 8),), jnp.float32),
        "screened": noise(own_keys[2], (QS, NG, NG), NG ** -0.5, 0.21875, ((0, 8),)),
        "coulomb": jnp.clip(jnp.exp(jax.random.uniform(own_keys[3], (NG,), jnp.float32, math.log(0.05), math.log(1.0))), 0.05, 1.0),
        "umklapp_map": jax.vmap(lambda own: jax.random.permutation(own, NG))(jax.random.split(keys[4], (STOPS + 1))).reshape((STOPS + 1, NG)).astype(jnp.int32),
    }


def make_amplitude(wave_rows, amp_rows):
    count = wave_rows.shape[0]
    valence = wave_rows[:, :NV].astype(jnp.float32)
    val_re = valence[:, :, 0]
    val_im = valence[:, :, 1]
    amps = amp_rows.reshape(count, 2, NV, NC)
    amp_re = amps[:, 0]
    amp_im = amps[:, 1]
    out_re = jnp.einsum('kvg,kvc->kcg', val_re, amp_re) - jnp.einsum('kvg,kvc->kcg', val_im, amp_im)
    out_im = jnp.einsum('kvg,kvc->kcg', val_re, amp_im) + jnp.einsum('kvg,kvc->kcg', val_im, amp_re)
    return jnp.stack([out_re, out_im], axis=2).astype(jnp.bfloat16)

def densities(wave_rows):
    wide = wave_rows.astype(jnp.float32)
    val_re = wide[:, :NV, 0][:, :, None, :]
    val_im = wide[:, :NV, 1][:, :, None, :]
    cond_re = wide[:, NV:, 0][:, None, :, :]
    cond_im = wide[:, NV:, 1][:, None, :, :]
    return (val_re * cond_re + val_im * cond_im, val_re * cond_im - val_im * cond_re)

def fold_exchange(dens_re, dens_im, amp_rows):
    count = amp_rows.shape[0]
    amps = amp_rows.reshape(count, 2, NV, NC)
    amp_re = amps[:, 0]
    amp_im = amps[:, 1]
    x_re = jnp.einsum('kvcg,kvc->g', dens_re, amp_re) + jnp.einsum('kvcg,kvc->g', dens_im, amp_im)
    x_im = jnp.einsum('kvcg,kvc->g', dens_re, amp_im) - jnp.einsum('kvcg,kvc->g', dens_im, amp_re)
    return (x_re, x_im)

def exchange_terms(dens_re, dens_im, x_re, x_im, coulomb):
    count = dens_re.shape[0]
    y_re = coulomb * x_re
    y_im = coulomb * x_im
    out_re = jnp.einsum('kvcg,g->kvc', dens_re, y_re) - jnp.einsum('kvcg,g->kvc', dens_im, y_im)
    out_im = jnp.einsum('kvcg,g->kvc', dens_re, y_im) + jnp.einsum('kvcg,g->kvc', dens_im, y_re)
    return jnp.stack([out_re, out_im], axis=1).reshape(count, -1)

def direct_fold(wave_rows, permuted, weight):
    valence = wave_rows[:, :NV].astype(jnp.float32)
    val_re = valence[:, :, 0][:, None, :, None, :]
    val_im = valence[:, :, 1][:, None, :, None, :]
    wide = permuted.astype(jnp.float32)
    ahat_re = wide[:, :NC, 0][None, :, None, :, :]
    ahat_im = wide[:, :NC, 1][None, :, None, :, :]
    cond_re = wide[:, NC:, 0]
    cond_im = wide[:, NC:, 1]
    y_re = val_re * ahat_re + val_im * ahat_im
    y_im = val_re * ahat_im - val_im * ahat_re
    stacked = jnp.stack([y_re, y_im], axis=4).astype(jnp.bfloat16)
    flat = stacked.reshape(-1, weight.shape[1])
    image = jnp.dot(flat, weight.T, preferred_element_type=jnp.float32).reshape(stacked.shape)
    z_re = image[:, :, :, :, 0]
    z_im = image[:, :, :, :, 1]
    e_re = jnp.einsum('kjvcg,jcg->kvg', z_re, cond_re) + jnp.einsum('kjvcg,jcg->kvg', z_im, cond_im)
    e_im = jnp.einsum('kjvcg,jcg->kvg', z_im, cond_re) - jnp.einsum('kjvcg,jcg->kvg', z_re, cond_im)
    return (e_re, e_im)

def finish(wave_rows, e_re, e_im):
    count = wave_rows.shape[0]
    cond = wave_rows[:, NV:].astype(jnp.float32)
    cond_re = cond[:, :, 0]
    cond_im = cond[:, :, 1]
    out_re = jnp.einsum('kcg,kvg->kvc', cond_re, e_re) - jnp.einsum('kcg,kvg->kvc', cond_im, e_im)
    out_im = jnp.einsum('kcg,kvg->kvc', cond_re, e_im) + jnp.einsum('kcg,kvg->kvc', cond_im, e_re)
    return jnp.stack([out_re, out_im], axis=1).reshape(count, -1)

def reference(wavefunc, haydock, screened, coulomb, umklapp_map):
    total = wavefunc.shape[0]
    amplitude = make_amplitude(wavefunc, haydock)
    partner = jnp.concatenate([amplitude, wavefunc[:, NV:]], axis=1)
    dens_re, dens_im = densities(wavefunc)
    x_re, x_im = fold_exchange(dens_re, dens_im, haydock)
    exchange = exchange_terms(dens_re, dens_im, x_re, x_im, coulomb) * (1.0 / (8.0 * math.sqrt(NG * NK)))
    scale_direct = -1.0 / (8.0 * math.sqrt(NG * KR * (STOPS + 1)))

    def per_block(block):
        rows_now = lax.dynamic_slice_in_dim(wavefunc, (block * KR).astype(jnp.int32), KR, 0)
        e_re = jnp.zeros((KR, NV, NG), jnp.float32)
        e_im = jnp.zeros((KR, NV, NG), jnp.float32)
        for stop_index in range(STOPS + 1):
            source = ((block - stop_index) % QS * KR).astype(jnp.int32)
            part_rows = lax.dynamic_slice_in_dim(partner, source, KR, 0)
            permuted = jnp.take(part_rows, umklapp_map[stop_index], axis=3)
            d_re, d_im = direct_fold(rows_now, permuted, screened[stop_index])
            e_re = e_re + d_re
            e_im = e_im + d_im
        return finish(rows_now, e_re, e_im)
    direct = lax.map(per_block, jnp.arange(QS, dtype=jnp.int32))
    direct = direct.reshape(total, -1) * scale_direct
    return direct + exchange
```

```python
import functools
import math

import jax
import jax.numpy as jnp
from jax import lax
from jax.experimental import pallas as pl
from jax.experimental.pallas import tpu as pltpu
from jax.sharding import PartitionSpec as P

NV = 8
NC = 8
STOPS = 2
BF = jnp.bfloat16
F32 = jnp.float32

OFFSET = {0: 0, 4: 0, 1: 1, 5: 1, 2: 2, 3: 2}
TARGETS = {0: (0, 1, 2, 3), 4: (4, 5, 6, 7), 1: (1, 0, 2, 3), 5: (5, 4, 6, 7), 2: (2, 0, 4, 6), 3: (3, 1, 5, 7)}
MATRIX_MOVES = ((0, 4), (1, 5), (2, 3))
BLOCKS = 8


def colour(edges, rounds):
    out, into, colours = {}, {}, {}
    for src, dst in edges:
        a = next(c for c in range(rounds) if c not in out.setdefault(src, {}))
        b = next(c for c in range(rounds) if c not in into.setdefault(dst, {}))
        if a != b:
            path, here, at_target, c = [], dst, True, a
            while True:
                other = (into if at_target else out).setdefault(here, {}).get(c)
                if other is None:
                    break
                path.append(((other, here) if at_target else (here, other), c))
                here, at_target, c = other, not at_target, (a if c == b else b)
            for (s, d), c in path:
                del out[s][c], into[d][c]
            for (s, d), c in path:
                c = a if c == b else b
                out[s][c], into[d][c], colours[s, d] = d, s, c
        out[src][a], into[dst][a], colours[src, dst] = dst, src, a
    return [tuple(sorted(e for e in colours if colours[e] == r)) for r in range(rounds)]


def plan():
    needs = {}
    for chip, targets in TARGETS.items():
        wanted = set(targets) | {(t - OFFSET[chip]) % BLOCKS for t in targets}
        needs[chip] = sorted(wanted - {chip})
    send = colour([(s, d) for d, srcs in needs.items() for s in srcs], 4)
    back = colour([(c, t) for c, targets in TARGETS.items() for t in targets[1:]], 3)
    table = []
    for chip in range(BLOCKS):
        if chip not in TARGETS:
            table.append([0, 0, 0, 0] + [0] * 8)
            continue
        slot = {chip: 0}
        for r, pairs in enumerate(send):
            for s, d in pairs:
                if d == chip:
                    slot[s] = r + 1
        order = [chip]
        for pairs in back:
            order += [d for s, d in pairs if s == chip]
        off = OFFSET[chip]
        moved = int(any(d == chip for _, d in MATRIX_MOVES))
        row = [1, off, moved, int(off == 0)]
        row += [slot[t] for t in order]
        row += [slot[(t - off) % BLOCKS] for t in order]
        table.append(row)
    return send, back, table


def iota(shape, dim):
    return lax.broadcasted_iota(jnp.int32, shape, dim)


def one(cond, sign=None):
    hit = jnp.where(cond, 1.0, 0.0)
    return hit if sign is None else hit * sign


def dot(a, b, dims=((1,), (0,)), **kw):
    return lax.dot_general(a, b, (dims, ((), ())), preferred_element_type=F32, **kw)


def message_kernel(who, flat, hay, mine, theirs):
    p = who[0]
    half = flat.shape[0] // 2
    share = hay.shape[0] // 2
    for ref, sel in ((mine, p), (theirs, 1 - p)):
        ref[0:half, :] = flat[pl.ds(pl.multiple_of(sel * half, 16), half), :]
        rows = jnp.where(sel == 0, hay[0:share, :], hay[share : 2 * share, :])
        hi = rows.astype(BF)
        lo = (rows - hi.astype(F32)).astype(BF)
        both = jnp.concatenate([hi, lo], axis=1).astype(F32)
        ref[half : half + 16, :] = jnp.zeros((16, flat.shape[1]), BF)
        ref[half : half + 16, 0:256] = jnp.concatenate([both, jnp.zeros((16 - share, 256), F32)], axis=0).astype(BF)


def prep_kernel(tab, who, umk, *refs):
    n_slots = 5
    msgs = refs[: 2 * n_slots]
    ap_ref, wt_ref, ua_ref, ub_ref, ch_ref, xs_ref, v_scr, c_scr, psi_scr = refs[2 * n_slots :]
    rows, planes = v_scr.shape[1], v_scr.shape[2]
    kr = rows // 16
    share = kr // 2
    gh = planes // 2
    p = who[0]

    @pl.when(tab[0] == 1)
    def _():
        for j in range(n_slots):
            for ref, sel in ((msgs[j], p), (msgs[n_slots + j], 1 - p)):
                for kk in range(share):
                    at = pl.multiple_of(sel * (16 * share) + 16 * kk, 16)
                    v_scr[j, pl.ds(at, 16), :] = ref[32 * kk : 32 * kk + 16, :]
                    c_scr[j, pl.ds(at, 16), :] = ref[32 * kk + 16 : 32 * kk + 32, :]
                psi_scr[j, pl.ds(pl.multiple_of(sel * 16, 16), 16), :] = ref[32 * share : 32 * share + 16, 0:256]

        row = umk[pl.ds(tab[1], 1), :]
        perm = one(iota((planes, planes), 0) == row).astype(BF)
        r = iota((rows, 32), 0)
        q = iota((rows, 32), 1)
        k = r // 16
        spread = one(q == jnp.where(k < share, k, 16 + k - share)).astype(BF)
        lane = iota((rows, 256), 1)
        keep = (lane % 8) == ((iota((rows, 256), 0) // 2) % 8)
        a = iota((128, rows), 0)
        b = iota((128, rows), 1)
        same_v = ((a // 8) % 8) == ((b // 2) % 8)
        part_a, part_b = a // 64, b % 2
        q0 = one(same_v & (part_a == part_b), jnp.where(part_a == 1, -1.0, 1.0)).astype(BF)
        q1 = one(same_v & (part_a != part_b)).astype(BF)
        rr = iota((rows, rows), 0)
        cc = iota((rows, rows), 1)
        block = (rr // 16) == (cc // 16)
        real_row = (rr % 2) == 0
        swap = one(rr == (cc + 1 - 2 * (cc % 2))).astype(BF)
        odd = (iota((rows, planes), 0) % 2) == 1

        xs_re = jnp.zeros((1, planes), F32)
        xs_im = jnp.zeros((1, planes), F32)
        for i in range(4):
            t = tab[4 + i]
            s = tab[8 + i]
            v = v_scr[s]
            c = c_scr[s]
            x = jnp.where(keep, dot(spread, psi_scr[s]), 0.0).astype(BF)
            both = []
            for piece in (x[:, 0:128], x[:, 128:256]):
                y0 = dot(piece, q0)
                y1 = dot(piece, q1)
                m_a = jnp.where(block, jnp.where(real_row, y0, y1), 0.0).astype(BF)
                m_b = jnp.where(block, jnp.where(real_row, y1, -y0), 0.0).astype(BF)
                both.append(jnp.concatenate([m_a, m_b], axis=0))
            amp = dot(both[0], v) + dot(both[1], v)
            cf = c.astype(F32)
            xs_re = xs_re + jnp.sum(cf * amp[:rows], axis=0, keepdims=True)
            xs_im = xs_im + jnp.sum(cf * amp[rows:], axis=0, keepdims=True)
            ap_ref[i] = dot(amp.astype(BF), perm).astype(BF)
            wp = dot(c, perm)
            wh = jnp.where(p == 0, wp[:, :gh], wp[:, gh:])
            wt_ref[i] = jnp.transpose(wh).astype(BF)
            vt = v_scr[t]
            vf = vt.astype(F32)
            ua_ref[i] = jnp.where(odd, -vf, vf).astype(BF)
            ub_ref[i] = dot(swap, vt).astype(BF)
            ct = c_scr[t]
            ch_ref[i] = jnp.where(p == 0, ct[:, :gh], ct[:, gh:])
        xs_ref[...] = jnp.concatenate([xs_re, xs_im], axis=0)


def main_kernel(scale_direct, scale_exchange, tab, who, w_own, w_in, ap, wt, ua, ub, ch, xs_own, xs_in, coulomb, *refs):
    outs, (f_scr,) = refs[:4], refs[4:]
    gh = w_own.shape[0]
    rows = ua.shape[1]
    kr = rows // 16
    p = who[0]
    a = iota((rows, 128), 0)
    b = iota((rows, 128), 1)
    same_v = ((a // 2) % 8) == ((b // 8) % 8)
    ra, rb = a % 2, b // 64
    qa = one(same_v & (ra == rb))
    qb = one(same_v & (ra != rb), jnp.where(rb == 0, -1.0, 1.0))
    real_row = (a % 2) == 0
    keep = (b % 8) == ((a // 2) % 8)
    rr = iota((rows, rows), 0)
    cc = iota((rows, rows), 1)
    block = (rr // 16) == (cc // 16)

    def item(i, w):
        step = 128
        for g in range(0, gh, step):
            wf = w[g : g + step, :].astype(F32)
            wti = wt[i, g : g + step, :]
            k_re = (wf * dot(wti, ap[i, 0:rows, :])).astype(BF)
            k_im = (wf * dot(wti, ap[i, rows : 2 * rows, :])).astype(BF)
            f = dot(k_re, ua[i], ((1,), (1,))) + dot(k_im, ub[i], ((1,), (1,)))
            f_scr[g : g + step, :] = f.astype(BF)
        return dot(ch[i], f_scr[...]) * scale_direct

    def finish(i, d):
        d = jnp.where(block, d, 0.0)
        z = jnp.where(
            real_row,
            dot(d, qa, precision=lax.Precision.HIGHEST),
            dot(d, qb, precision=lax.Precision.HIGHEST),
        )
        z = jnp.where(keep, z, 0.0)
        outs[i][...] = jnp.sum(z.reshape(kr, 16, 128), axis=1)

    def exchange(i):
        y_re = coulomb[...] * (xs_own[0:1, :] + xs_in[0:1, :]) * scale_exchange
        y_im = coulomb[...] * (xs_own[1:2, :] + xs_in[1:2, :]) * scale_exchange
        f = (ua[i].astype(F32) * y_re + ub[i].astype(F32) * y_im).astype(BF)
        fh = jnp.where(p == 0, f[:, :gh], f[:, gh:])
        return dot(ch[i], fh, ((1,), (1,)))

    @pl.when(tab[0] == 0)
    def _():
        for o in outs:
            o[...] = jnp.zeros_like(o)

    for moved in (0, 1):

        @pl.when((tab[0] == 1) & (tab[2] == moved))
        def _(w=(w_own, w_in)[moved]):
            for i in range(4):
                d = item(i, w)
                d = d + jnp.where(tab[3] == 1, exchange(i), 0.0)
                finish(i, d)


VM = pl.BlockSpec(memory_space=pltpu.VMEM)
SM = pl.BlockSpec(memory_space=pltpu.SMEM)


def call(kernel, outs, ins, scratch=(), flops=0, limit=48 << 20):
    specs = [SM if x.dtype == jnp.int32 and x.ndim == 1 else VM for x in ins]
    moved = sum(math.prod(x.shape) * x.dtype.itemsize for x in (*ins, *outs))
    return pl.pallas_call(
        kernel,
        out_shape=outs,
        in_specs=specs,
        out_specs=[VM] * len(outs),
        scratch_shapes=list(scratch),
        compiler_params=pltpu.CompilerParams(vmem_limit_bytes=limit),
        cost_estimate=pl.CostEstimate(flops=flops, bytes_accessed=moved, transcendentals=0),
    )(*ins)


def eight_blocks(wavefunc, haydock, screened, coulomb, umklapp_map):
    send, back, table = plan()
    kr, nb, _, planes = wavefunc.shape
    rows = kr * 16
    gh = planes // 2
    member = lax.axis_index("pair").astype(jnp.int32)
    me = lax.axis_index("blk")
    tab = jnp.asarray(table, jnp.int32)[me]
    who = member.reshape(1)

    def over_blocks(x, pairs):
        return lax.ppermute(x, "blk", pairs)

    def swap(x):
        return lax.ppermute(x, "pair", [(0, 1), (1, 0)])

    w_own = lax.dynamic_slice_in_dim(screened[0], member * gh, gh, 0)
    w_in = over_blocks(w_own, MATRIX_MOVES)
    flat = wavefunc.reshape(kr * nb * 2, planes)
    shape = jax.ShapeDtypeStruct
    msg = shape((rows + 16, planes), BF)
    mine, theirs = call(message_kernel, [msg, msg], [who, flat, haydock])
    got = [over_blocks(mine, pairs) for pairs in send]
    other = [swap(x) for x in got]
    ap, wt, ua, ub, ch, xs = call(
        prep_kernel,
        [
            shape((4, 2 * rows, planes), BF),
            shape((4, gh, rows), BF),
            shape((4, rows, planes), BF),
            shape((4, rows, planes), BF),
            shape((4, rows, gh), BF),
            shape((2, planes), F32),
        ],
        [tab, who, umklapp_map, mine, *got, theirs, *other],
        scratch=[pltpu.VMEM((5, rows, planes), BF), pltpu.VMEM((5, rows, planes), BF), pltpu.VMEM((5, 32, 256), BF)],
        flops=4 * 2 * planes * planes * rows * 3,
    )
    xs_in = over_blocks(xs, ((0, 4), (4, 0)))
    total_k = kr * lax.axis_size("blk")
    scale_exchange = 1.0 / (8.0 * math.sqrt(planes * total_k))
    scale_direct = -1.0 / (8.0 * math.sqrt(planes * kr * (STOPS + 1)))
    result = shape((kr, 128), F32)
    outs = call(
        functools.partial(main_kernel, scale_direct, scale_exchange),
        [result] * 4,
        [tab, who, w_own, w_in, ap, wt, ua, ub, ch, xs, xs_in, coulomb.reshape(1, planes)],
        scratch=[pltpu.VMEM((gh, rows), BF)],
        flops=4 * 8 * gh * planes * rows,
    )
    total = outs[0]
    for piece, pairs in zip(outs[1:], back, strict=True):
        total = total + over_blocks(piece, pairs)
    return total + swap(total)


def from_root(block, axis, holder):
    block = jnp.where(lax.axis_index(axis) == holder, block, jnp.zeros_like(block))
    return lax.psum(block, axis)


def from_behind(value, axis, by):
    devices = lax.axis_size(axis)
    return lax.ppermute(value, axis, [(i, (i + by) % devices) for i in range(devices)])


def make_amplitude(wave_rows, amp_rows):
    count = wave_rows.shape[0]
    valence = wave_rows[:, :NV].astype(jnp.float32)
    val_re = valence[:, :, 0]
    val_im = valence[:, :, 1]
    amps = amp_rows.reshape(count, 2, NV, NC)
    amp_re = amps[:, 0]
    amp_im = amps[:, 1]
    out_re = jnp.einsum("kvg,kvc->kcg", val_re, amp_re) - jnp.einsum("kvg,kvc->kcg", val_im, amp_im)
    out_im = jnp.einsum("kvg,kvc->kcg", val_re, amp_im) + jnp.einsum("kvg,kvc->kcg", val_im, amp_re)
    return jnp.stack([out_re, out_im], axis=2).astype(jnp.bfloat16)


def densities(wave_rows):
    wide = wave_rows.astype(jnp.float32)
    val_re = wide[:, :NV, 0][:, :, None, :]
    val_im = wide[:, :NV, 1][:, :, None, :]
    cond_re = wide[:, NV:, 0][:, None, :, :]
    cond_im = wide[:, NV:, 1][:, None, :, :]
    return (val_re * cond_re + val_im * cond_im, val_re * cond_im - val_im * cond_re)


def fold_exchange(dens_re, dens_im, amp_rows):
    count = amp_rows.shape[0]
    amps = amp_rows.reshape(count, 2, NV, NC)
    amp_re = amps[:, 0]
    amp_im = amps[:, 1]
    x_re = jnp.einsum("kvcg,kvc->g", dens_re, amp_re) + jnp.einsum("kvcg,kvc->g", dens_im, amp_im)
    x_im = jnp.einsum("kvcg,kvc->g", dens_re, amp_im) - jnp.einsum("kvcg,kvc->g", dens_im, amp_re)
    return (x_re, x_im)


def exchange_terms(dens_re, dens_im, x_re, x_im, coulomb):
    count = dens_re.shape[0]
    y_re = coulomb * x_re
    y_im = coulomb * x_im
    out_re = jnp.einsum("kvcg,g->kvc", dens_re, y_re) - jnp.einsum("kvcg,g->kvc", dens_im, y_im)
    out_im = jnp.einsum("kvcg,g->kvc", dens_re, y_im) + jnp.einsum("kvcg,g->kvc", dens_im, y_re)
    return jnp.stack([out_re, out_im], axis=1).reshape(count, -1)


def direct_fold(wave_rows, permuted, weight):
    valence = wave_rows[:, :NV].astype(jnp.float32)
    val_re = valence[:, :, 0][:, None, :, None, :]
    val_im = valence[:, :, 1][:, None, :, None, :]
    wide = permuted.astype(jnp.float32)
    ahat_re = wide[:, :NC, 0][None, :, None, :, :]
    ahat_im = wide[:, :NC, 1][None, :, None, :, :]
    cond_re = wide[:, NC:, 0]
    cond_im = wide[:, NC:, 1]
    y_re = val_re * ahat_re + val_im * ahat_im
    y_im = val_re * ahat_im - val_im * ahat_re
    stacked = jnp.stack([y_re, y_im], axis=4).astype(jnp.bfloat16)
    flat = stacked.reshape(-1, weight.shape[1])
    image = lax.dot_general(flat, weight, (((1,), (1,)), ((), ())), preferred_element_type=jnp.float32)
    image = image.reshape(stacked.shape)
    z_re = image[:, :, :, :, 0]
    z_im = image[:, :, :, :, 1]
    e_re = jnp.einsum("kjvcg,jcg->kvg", z_re, cond_re) + jnp.einsum("kjvcg,jcg->kvg", z_im, cond_im)
    e_im = jnp.einsum("kjvcg,jcg->kvg", z_im, cond_re) - jnp.einsum("kjvcg,jcg->kvg", z_re, cond_im)
    return (e_re, e_im)


def finish_direct(wave_rows, e_re, e_im):
    count = wave_rows.shape[0]
    cond = wave_rows[:, NV:].astype(jnp.float32)
    cond_re = cond[:, :, 0]
    cond_im = cond[:, :, 1]
    out_re = jnp.einsum("kcg,kvg->kvc", cond_re, e_re) - jnp.einsum("kcg,kvg->kvc", cond_im, e_im)
    out_im = jnp.einsum("kcg,kvg->kvc", cond_re, e_im) + jnp.einsum("kcg,kvg->kvc", cond_im, e_re)
    return jnp.stack([out_re, out_im], axis=1).reshape(count, -1)


def any_blocks(wavefunc, haydock, screened, coulomb, umklapp_map):
    row_count = wavefunc.shape[0]
    plane_count = wavefunc.shape[3]
    share = row_count // lax.axis_size("pair")
    member = lax.axis_index("pair")
    amplitude = make_amplitude(wavefunc, haydock)
    partner = jnp.concatenate([amplitude, wavefunc[:, NV:]], axis=1)
    current = lax.dynamic_slice_in_dim(partner, member * share, share, 0)
    full_re, full_im = densities(wavefunc)
    share_re = lax.dynamic_slice_in_dim(full_re, member * share, share, 0)
    share_im = lax.dynamic_slice_in_dim(full_im, member * share, share, 0)
    hay_share = lax.dynamic_slice_in_dim(haydock, member * share, share, 0)
    x_re, x_im = fold_exchange(share_re, share_im, hay_share)
    x_re, x_im = lax.psum((x_re, x_im), ("blk", "pair"))
    total_k = row_count * lax.axis_size("blk")
    exchange = exchange_terms(full_re, full_im, x_re, x_im, coulomb) * (
        1.0 / (8.0 * math.sqrt(plane_count * total_k))
    )
    scale_direct = -1.0 / (8.0 * math.sqrt(plane_count * row_count * (STOPS + 1)))
    e_re = jnp.zeros((row_count, NV, plane_count), jnp.float32)
    e_im = jnp.zeros((row_count, NV, plane_count), jnp.float32)
    for stop_index in range(STOPS + 1):
        if stop_index > 0:
            current = from_behind(current, "blk", 1)
        weight = from_root(screened[0], "blk", stop_index)
        permuted = jnp.take(current, umklapp_map[stop_index], axis=3)
        d_re, d_im = direct_fold(wavefunc, permuted, weight)
        e_re = e_re + d_re
        e_im = e_im + d_im
    direct = finish_direct(wavefunc, e_re, e_im) * scale_direct
    return lax.psum(direct, "pair") + exchange


def solution(mesh):
    placed = (
        P(("grp", "blk"), None, None, None),
        P(("grp", "blk"), None),
        P(("grp", "blk"), None, None),
        P("grp"),
        P(),
    )
    body = eight_blocks if mesh.shape["blk"] == BLOCKS and mesh.shape["pair"] == 2 else any_blocks
    return jax.shard_map(body, mesh=mesh, in_specs=placed, out_specs=P(("grp", "blk"), None), check_vma=False)
```

```python
import functools
import math

import jax
import jax.numpy as jnp
from jax import lax
from jax.experimental import pallas as pl
from jax.experimental.pallas import tpu as pltpu
from jax.sharding import PartitionSpec as P

NV = 8
NC = 8
STOPS = 2
BF = jnp.bfloat16
F32 = jnp.float32

BLOCKS = 8
OFFSET = {0: 0, 4: 0, 1: 1, 5: 1, 2: 2, 3: 2}
TARGETS = {
    (0, 0): (0, 1), (0, 1): (2, 3),
    (1, 0): (1, 0), (1, 1): (3, 2),
    (2, 0): (2, 0), (2, 1): (6, 4),
    (3, 0): (3, 1), (3, 1): (7, 5),
    (4, 0): (4, 5), (4, 1): (7, 6),
    (5, 0): (5, 4), (5, 1): (6, 7),
}
MATRIX_MOVES = ((0, 4), (1, 5), (2, 3))
FETCH = {
    (0, 0): (1, None), (0, 1): (2, 3),
    (1, 0): (0, 7), (1, 1): (3, 2),
    (2, 0): (None, 0), (2, 1): (6, 4),
    (3, 0): (None, 1), (3, 1): (7, 5),
    (4, 0): (5, None), (4, 1): (6, 7),
    (5, 0): (4, 3), (5, 1): (7, 6),
}
SUMS = ((0, 4), (4, 0))


def pick_cores(pairs, fixed):
    taken, out = {}, []
    for src, dst in pairs:
        chip, core = (src, dst[1]) if fixed == "dst" else (dst, src[1])
        used = taken.setdefault(chip, set())
        core = core if core not in used else 1 - core
        assert core not in used
        used.add(core)
        a, b = ((chip, core), dst) if fixed == "dst" else (src, (chip, core))
        out.append((a[0] * 2 + a[1], b[0] * 2 + b[1]))
    return out


def plan():
    fetch = [pick_cores([(got[r], at) for at, got in FETCH.items() if got[r] is not None], "dst") for r in range(2)]
    home = [
        pick_cores([(at, t[1] if at[1] == 0 else t[0]) for at, t in TARGETS.items()], "src"),
        pick_cores([(at, t[1]) for at, t in TARGETS.items() if at[1] == 1], "src"),
    ]
    table = {}
    for chip, core in TARGETS:
        first, second = FETCH[chip, core]
        held = [chip, first, FETCH[chip, 1 - core][0], second]
        off = OFFSET[chip]
        moved = int(any(d == chip for _, d in MATRIX_MOVES))
        row = [1, off, moved, int(off == 0)]
        row += [held.index(t) for t in TARGETS[chip, core]]
        row += [held.index((t - off) % BLOCKS) for t in TARGETS[chip, core]]
        table[chip, core] = row
    return fetch, home, table


FETCH_ROUNDS, HOME_ROUNDS, TABLE = plan()


def entry(who, column):
    value = jnp.int32(0)
    for b in range(BLOCKS):
        if (b, 0) in TABLE and (TABLE[b, 0][column] or TABLE[b, 1][column]):
            here = jnp.where(who[1] == 0, TABLE[b, 0][column], TABLE[b, 1][column])
            value = jnp.where(who[0] == b, here, value)
    return value


def iota(shape, dim):
    return lax.broadcasted_iota(jnp.int32, shape, dim)


def one(cond, sign=None):
    hit = jnp.where(cond, 1.0, 0.0)
    return hit if sign is None else hit * sign


def dot(a, b, dims=((1,), (0,)), **kw):
    return lax.dot_general(a, b, (dims, ((), ())), preferred_element_type=F32, **kw)


def message_kernel(flat, hay, mine):
    rows, planes = flat.shape
    kr = hay.shape[0]
    mine[0:rows, :] = flat[...]
    h = hay[...]
    hi = h.astype(BF)
    lo = (h - hi.astype(F32)).astype(BF)
    both = jnp.concatenate([hi.astype(F32), lo.astype(F32)], axis=1)
    mine[rows : rows + 16, :] = jnp.zeros((16, planes), BF)
    mine[rows : rows + 16, 0:256] = jnp.concatenate([both, jnp.zeros((16 - kr, 256), F32)], axis=0).astype(BF)


def perm_kernel(who, umk, screened, perm, w_half):
    planes = perm.shape[0]
    gh = w_half.shape[0]
    w_half[...] = screened[pl.ds(pl.multiple_of(who[1] * gh, 128), gh), :]
    row = umk[pl.ds(entry(who, 1), 1), :]
    perm[...] = one(iota((planes, planes), 0) == row).astype(BF)


def amplitude(msg, v, c):
    rows = v.shape[0]
    for k in range(rows // 16):
        v[16 * k : 16 * k + 16, :] = msg[32 * k : 32 * k + 16, :]
        c[16 * k : 16 * k + 16, :] = msg[32 * k + 16 : 32 * k + 32, :]
    spread = one(iota((rows, 16), 1) == iota((rows, 16), 0) // 16).astype(BF)
    keep = (iota((rows, 256), 1) % 8) == ((iota((rows, 256), 0) // 2) % 8)
    a = iota((128, rows), 0)
    b = iota((128, rows), 1)
    same_v = ((a // 8) % 8) == ((b // 2) % 8)
    part_a, part_b = a // 64, b % 2
    q0 = one(same_v & (part_a == part_b), jnp.where(part_a == 1, -1.0, 1.0))
    q1 = one(same_v & (part_a != part_b))
    q = jnp.concatenate([q0, q1], axis=1).astype(BF)
    block = (iota((rows, rows), 0) // 16) == (iota((rows, rows), 1) // 16)
    real_row = (iota((rows, rows), 0) % 2) == 0
    x = jnp.where(keep, dot(spread, msg[2 * rows : 2 * rows + 16, 0:256]), 0.0).astype(BF)
    pieces = []
    for piece in (x[:, 0:128], x[:, 128:256]):
        y = dot(piece, q)
        y0, y1 = y[:, :rows], y[:, rows:]
        pieces.append(jnp.where(block, jnp.where(real_row, y0, y1), 0.0).astype(BF))
        pieces.append(jnp.where(block, jnp.where(real_row, y1, -y0), 0.0).astype(BF))
    bands = v[...]
    return dot(pieces[0], bands) + dot(pieces[2], bands), dot(pieces[1], bands) + dot(pieces[3], bands)


def sums(c, amp, turned):
    cf = c[...].astype(F32)
    return jnp.concatenate([jnp.sum(cf * amp, axis=0, keepdims=True), jnp.sum(cf * turned, axis=0, keepdims=True)], axis=0)


def turn_matrix(rows):
    rr, cc = iota((rows, rows), 0), iota((rows, rows), 1)
    pairs = one(rr == (cc + 1 - 2 * (cc % 2)))
    return jnp.where(rr % 2 == 0, pairs, -pairs).astype(BF)


def permute(a, c, perm, ap_refs, wt_refs, cb_refs):
    n = len(ap_refs)
    rows = c.shape[0] // n
    turn = turn_matrix(rows)
    wp = dot(c[...], perm[...])
    ap = dot(a[...], perm[...]).astype(BF)
    for j in range(n):
        part = slice(j * rows, (j + 1) * rows)
        ap_refs[j][0:rows, :] = ap[part]
        ap_refs[j][rows : 2 * rows, :] = dot(turn, ap[part]).astype(BF)
        wt_refs[j][...] = jnp.transpose(wp[part]).astype(BF)
        cb_refs[j][...] = (-dot(turn, c[part, :])).astype(BF)


def prep_kernel(n, who, perm, *refs):
    msgs, (ap, wt, v, ca, cb, xs, a_scr) = refs[:n], refs[n:]
    rows, planes = v.shape[1:]

    @pl.when(entry(who, 0) == 1)
    def _():
        total = jnp.zeros((2, planes), F32)
        for j in range(n):
            mine = pl.ds(j * rows, rows)
            amp, turned = amplitude(msgs[j], v.at[j], ca.at[mine])
            total = total + sums(ca.at[mine], amp, turned)
            a_scr[mine, :] = amp.astype(BF)
        xs[...] = total
        each = range(n)
        permute(a_scr, ca, perm, [ap.at[j] for j in each], [wt.at[j] for j in each], [cb.at[j] for j in each])

    @pl.when(entry(who, 0) == 0)
    def _():
        xs[...] = jnp.zeros_like(xs)


def last_kernel(who, msg, xs_0, xs_1, v, c, a, xs):
    @pl.when(entry(who, 0) == 1)
    def _():
        amp, turned = amplitude(msg, v, c)
        a[...] = amp.astype(BF)
        xs[...] = xs_0[...] + xs_1[...] + sums(c, amp, turned)

    @pl.when(entry(who, 0) == 0)
    def _():
        xs[...] = jnp.zeros_like(xs)


def main_kernel(who, perm, w_own, w_in, w_swapped, *refs):
    own, two, (v_3, c_3, a_3) = refs[0:5], refs[5:10], refs[10:13]
    d_ref, vt_ref, ca_ref, cb_ref, wf, ap_3, wt_3, cb_3, ap_scr, wt_scr = refs[13:]
    rows, planes = v_3.shape
    gh = planes // 2
    p = who[1]

    @pl.when((entry(who, 0) == 1) & (entry(who, 2) == 0))
    def _():
        wf[...] = w_own[...].astype(F32)

    @pl.when((entry(who, 0) == 1) & (entry(who, 2) == 1))
    def _():
        wf[pl.ds(pl.multiple_of(p * gh, 128), gh), :] = w_in[...].astype(F32)
        wf[pl.ds(pl.multiple_of((1 - p) * gh, 128), gh), :] = w_swapped[...].astype(F32)

    @pl.when(entry(who, 0) == 1)
    def _():
        permute(a_3, c_3, perm, [ap_3], [wt_3], [cb_3])

    def held(slot):
        if slot == 3:
            return ap_3, wt_3, v_3, c_3, cb_3
        ap, wt, v, ca, cb = own if slot == 0 else two
        j = max(slot - 1, 0)
        return ap.at[j], wt.at[j], v.at[j], ca.at[pl.ds(j * rows, rows)], cb.at[j]

    for i in range(2):
        for slot in range(4):

            @pl.when((entry(who, 0) == 1) & (entry(who, 4 + i) == slot))
            def _(i=i, slot=slot):
                _, _, v, ca, cb = held(slot)
                vt_ref[i], ca_ref[i], cb_ref[i] = v[...], ca[...], cb[...]

            @pl.when((entry(who, 0) == 1) & (entry(who, 6 + i) == slot))
            def _(i=i, slot=slot):
                ap, wt = held(slot)[:2]
                ap_scr[i], wt_scr[i] = ap[...], wt[...]

    @pl.when(entry(who, 0) == 1)
    def _():
        kernels = []
        for i in range(2):
            for h in range(2):
                w = wf[h * gh : (h + 1) * gh, :]
                left = wt_scr[i, h * gh : (h + 1) * gh, :]
                k_re = (w * dot(left, ap_scr[i, 0:rows, :])).astype(BF)
                k_im = (w * dot(left, ap_scr[i, rows : 2 * rows, :])).astype(BF)
                kernels.append((k_re, k_im))
        sides = []
        for i in range(2):
            y = None
            for h in range(2):
                k_re, k_im = kernels[2 * i + h]
                part = slice(h * gh, (h + 1) * gh)
                z = dot(ca_ref[i, :, part], k_re) + dot(cb_ref[i, :, part], k_im)
                y = z if y is None else y + z
            sides.append(y.astype(BF))
        for i, y in enumerate(sides):
            d_ref[i] = dot(y, vt_ref[i], ((1,), (1,)))


def finish_kernel(scale_direct, scale_exchange, who, d_ref, v, ca, cb, *refs):
    xs, xs_swapped, xs_in, xs_in_swapped, coulomb, stays, goes_1, goes_2 = refs
    rows = v.shape[1]
    kr = rows // 16
    p = who[1]
    a = iota((rows, 128), 0)
    b = iota((rows, 128), 1)
    same_v = ((a // 2) % 8) == ((b // 8) % 8)
    ra, rb = a % 2, b // 64
    qa = one(same_v & (ra == rb), jnp.where(rb == 1, -1.0, 1.0))
    qb = one(same_v & (ra != rb))
    q = jnp.concatenate([qa, qb], axis=1)
    real_row = (a % 2) == 0
    keep = (b % 8) == ((a // 2) % 8)
    block = (iota((rows, rows), 0) // 16) == (iota((rows, rows), 1) // 16)

    def result(d):
        d = jnp.where(block, d, 0.0)
        z = dot(d, q, precision=lax.Precision.HIGHEST)
        z = jnp.where(keep, jnp.where(real_row, z[:, :128], z[:, 128:]), 0.0)
        return jnp.sum(z.reshape(kr, 16, 128), axis=1)

    def store(one_, two):
        r1, r2 = result(one_), result(two)
        core_0 = p == 0
        stays[...] = jnp.where(core_0, r1, 0.0)
        goes_1[...] = jnp.where(core_0, r2, r1)
        goes_2[...] = jnp.where(core_0, 0.0, r2)

    @pl.when(entry(who, 0) == 0)
    def _():
        for o in (stays, goes_1, goes_2):
            o[...] = jnp.zeros_like(o)

    @pl.when((entry(who, 0) == 1) & (entry(who, 3) == 0))
    def _():
        store(*(d_ref[i] * scale_direct for i in range(2)))

    @pl.when((entry(who, 0) == 1) & (entry(who, 3) == 1))
    def _():
        total = jnp.where(p == 1, xs[...] + xs_in[...], xs_swapped[...] + xs_in_swapped[...])
        y = coulomb[...] * total * scale_exchange
        both = []
        for i in range(2):
            side = (ca[i].astype(F32) * y[0:1] + cb[i].astype(F32) * y[1:2]).astype(BF)
            both.append(d_ref[i] * scale_direct + dot(side, v[i], ((1,), (1,))))
        store(*both)


VM = pl.BlockSpec(memory_space=pltpu.VMEM)
SM = pl.BlockSpec(memory_space=pltpu.SMEM)


def call(kernel, outs, ins, scratch=(), limit=24 << 20):
    moved = sum(math.prod(x.shape) * x.dtype.itemsize for x in (*ins, *outs))
    specs = [SM if x.dtype == jnp.int32 and x.ndim == 1 else VM for x in ins]
    return pl.pallas_call(
        kernel,
        out_shape=outs,
        in_specs=specs,
        out_specs=[VM] * len(outs),
        scratch_shapes=list(scratch),
        compiler_params=pltpu.CompilerParams(vmem_limit_bytes=limit),
        cost_estimate=pl.CostEstimate(flops=0, bytes_accessed=moved, transcendentals=0),
    )(*ins)


def eight_blocks(wavefunc, haydock, screened, coulomb, umklapp_map):
    kr, nb, _, planes = wavefunc.shape
    rows = kr * 16
    gh = planes // 2
    shape = jax.ShapeDtypeStruct
    member = lax.axis_index("pair").astype(jnp.int32)
    who = jnp.stack([lax.axis_index("blk").astype(jnp.int32), member])

    def over_cores(x, pairs):
        return lax.ppermute(x, ("blk", "pair"), pairs)

    def swap(x):
        return lax.ppermute(x, "pair", [(0, 1), (1, 0)])

    def prep(perm, msgs):
        n = len(msgs)
        outs = [
            shape((n, 2 * rows, planes), BF),
            shape((n, planes, rows), BF),
            shape((n, rows, planes), BF),
            shape((n * rows, planes), BF),
            shape((n, rows, planes), BF),
            shape((2, planes), F32),
        ]
        return call(
            functools.partial(prep_kernel, n), outs, [who, perm, *msgs], scratch=[pltpu.VMEM((n * rows, planes), BF)]
        )

    flat = wavefunc.reshape(kr * nb * 2, planes)
    perm, w_half = call(
        perm_kernel, [shape((planes, planes), BF), shape((gh, planes), BF)], [who, umklapp_map, screened[0]]
    )
    w_in = lax.ppermute(w_half, "blk", MATRIX_MOVES)
    (mine,) = call(message_kernel, [shape((2 * rows + 16, planes), BF)], [flat, haydock])
    got_1 = over_cores(mine, FETCH_ROUNDS[0])
    own = prep(perm, [mine])
    got_1, mine, *own = lax.optimization_barrier((got_1, mine, *own))
    got_2 = over_cores(mine, FETCH_ROUNDS[1])
    two = prep(perm, [got_1, swap(got_1)])
    got_2, w_in, *two = lax.optimization_barrier((got_2, w_in, *two))
    bands = shape((rows, planes), BF)
    v_3, c_3, a_3, xs = call(
        last_kernel, [bands, bands, bands, shape((2, planes), F32)], [who, got_2, own[5], two[5]]
    )
    xs_in = lax.ppermute(xs, "blk", SUMS)
    xs_all = [xs, swap(xs), xs_in, swap(xs_in)]
    total_k = kr * lax.axis_size("blk")
    scale_exchange = 1.0 / (8.0 * math.sqrt(planes * total_k))
    scale_direct = -1.0 / (8.0 * math.sqrt(planes * kr * (STOPS + 1)))
    item = shape((2, rows, planes), BF)
    d, v, ca, cb = call(
        main_kernel,
        [shape((2, rows, rows), F32), item, item, item],
        [who, perm, screened[0], w_in, swap(w_in), *own[:5], *two[:5], v_3, c_3, a_3],
        scratch=[
            pltpu.VMEM((planes, planes), F32),
            pltpu.VMEM((2 * rows, planes), BF),
            pltpu.VMEM((planes, rows), BF),
            pltpu.VMEM((rows, planes), BF),
            pltpu.VMEM((2, 2 * rows, planes), BF),
            pltpu.VMEM((2, planes, rows), BF),
        ],
    )
    stays, goes_1, goes_2 = call(
        functools.partial(finish_kernel, scale_direct, scale_exchange),
        [shape((kr, 128), F32)] * 3,
        [who, d, v, ca, cb, *xs_all, coulomb.reshape(1, planes)],
    )
    total = stays + over_cores(goes_1, HOME_ROUNDS[0]) + over_cores(goes_2, HOME_ROUNDS[1])
    return total + swap(total)


def from_root(block, axis, holder):
    block = jnp.where(lax.axis_index(axis) == holder, block, jnp.zeros_like(block))
    return lax.psum(block, axis)


def from_behind(value, axis, by):
    devices = lax.axis_size(axis)
    return lax.ppermute(value, axis, [(i, (i + by) % devices) for i in range(devices)])


def make_amplitude(wave_rows, amp_rows):
    count = wave_rows.shape[0]
    valence = wave_rows[:, :NV].astype(jnp.float32)
    val_re = valence[:, :, 0]
    val_im = valence[:, :, 1]
    amps = amp_rows.reshape(count, 2, NV, NC)
    amp_re = amps[:, 0]
    amp_im = amps[:, 1]
    out_re = jnp.einsum("kvg,kvc->kcg", val_re, amp_re) - jnp.einsum("kvg,kvc->kcg", val_im, amp_im)
    out_im = jnp.einsum("kvg,kvc->kcg", val_re, amp_im) + jnp.einsum("kvg,kvc->kcg", val_im, amp_re)
    return jnp.stack([out_re, out_im], axis=2).astype(jnp.bfloat16)


def densities(wave_rows):
    wide = wave_rows.astype(jnp.float32)
    val_re = wide[:, :NV, 0][:, :, None, :]
    val_im = wide[:, :NV, 1][:, :, None, :]
    cond_re = wide[:, NV:, 0][:, None, :, :]
    cond_im = wide[:, NV:, 1][:, None, :, :]
    return (val_re * cond_re + val_im * cond_im, val_re * cond_im - val_im * cond_re)


def fold_exchange(dens_re, dens_im, amp_rows):
    count = amp_rows.shape[0]
    amps = amp_rows.reshape(count, 2, NV, NC)
    amp_re = amps[:, 0]
    amp_im = amps[:, 1]
    x_re = jnp.einsum("kvcg,kvc->g", dens_re, amp_re) + jnp.einsum("kvcg,kvc->g", dens_im, amp_im)
    x_im = jnp.einsum("kvcg,kvc->g", dens_re, amp_im) - jnp.einsum("kvcg,kvc->g", dens_im, amp_re)
    return (x_re, x_im)


def exchange_terms(dens_re, dens_im, x_re, x_im, coulomb):
    count = dens_re.shape[0]
    y_re = coulomb * x_re
    y_im = coulomb * x_im
    out_re = jnp.einsum("kvcg,g->kvc", dens_re, y_re) - jnp.einsum("kvcg,g->kvc", dens_im, y_im)
    out_im = jnp.einsum("kvcg,g->kvc", dens_re, y_im) + jnp.einsum("kvcg,g->kvc", dens_im, y_re)
    return jnp.stack([out_re, out_im], axis=1).reshape(count, -1)


def direct_fold(wave_rows, permuted, weight):
    valence = wave_rows[:, :NV].astype(jnp.float32)
    val_re = valence[:, :, 0][:, None, :, None, :]
    val_im = valence[:, :, 1][:, None, :, None, :]
    wide = permuted.astype(jnp.float32)
    ahat_re = wide[:, :NC, 0][None, :, None, :, :]
    ahat_im = wide[:, :NC, 1][None, :, None, :, :]
    cond_re = wide[:, NC:, 0]
    cond_im = wide[:, NC:, 1]
    y_re = val_re * ahat_re + val_im * ahat_im
    y_im = val_re * ahat_im - val_im * ahat_re
    stacked = jnp.stack([y_re, y_im], axis=4).astype(jnp.bfloat16)
    flat = stacked.reshape(-1, weight.shape[1])
    image = lax.dot_general(flat, weight, (((1,), (1,)), ((), ())), preferred_element_type=jnp.float32)
    image = image.reshape(stacked.shape)
    z_re = image[:, :, :, :, 0]
    z_im = image[:, :, :, :, 1]
    e_re = jnp.einsum("kjvcg,jcg->kvg", z_re, cond_re) + jnp.einsum("kjvcg,jcg->kvg", z_im, cond_im)
    e_im = jnp.einsum("kjvcg,jcg->kvg", z_im, cond_re) - jnp.einsum("kjvcg,jcg->kvg", z_re, cond_im)
    return (e_re, e_im)


def finish_direct(wave_rows, e_re, e_im):
    count = wave_rows.shape[0]
    cond = wave_rows[:, NV:].astype(jnp.float32)
    cond_re = cond[:, :, 0]
    cond_im = cond[:, :, 1]
    out_re = jnp.einsum("kcg,kvg->kvc", cond_re, e_re) - jnp.einsum("kcg,kvg->kvc", cond_im, e_im)
    out_im = jnp.einsum("kcg,kvg->kvc", cond_re, e_im) + jnp.einsum("kcg,kvg->kvc", cond_im, e_re)
    return jnp.stack([out_re, out_im], axis=1).reshape(count, -1)


def any_blocks(wavefunc, haydock, screened, coulomb, umklapp_map):
    row_count = wavefunc.shape[0]
    plane_count = wavefunc.shape[3]
    share = row_count // lax.axis_size("pair")
    member = lax.axis_index("pair")
    amplitude = make_amplitude(wavefunc, haydock)
    partner = jnp.concatenate([amplitude, wavefunc[:, NV:]], axis=1)
    current = lax.dynamic_slice_in_dim(partner, member * share, share, 0)
    full_re, full_im = densities(wavefunc)
    share_re = lax.dynamic_slice_in_dim(full_re, member * share, share, 0)
    share_im = lax.dynamic_slice_in_dim(full_im, member * share, share, 0)
    hay_share = lax.dynamic_slice_in_dim(haydock, member * share, share, 0)
    x_re, x_im = fold_exchange(share_re, share_im, hay_share)
    x_re, x_im = lax.psum((x_re, x_im), ("blk", "pair"))
    total_k = row_count * lax.axis_size("blk")
    exchange = exchange_terms(full_re, full_im, x_re, x_im, coulomb) * (
        1.0 / (8.0 * math.sqrt(plane_count * total_k))
    )
    scale_direct = -1.0 / (8.0 * math.sqrt(plane_count * row_count * (STOPS + 1)))
    e_re = jnp.zeros((row_count, NV, plane_count), jnp.float32)
    e_im = jnp.zeros((row_count, NV, plane_count), jnp.float32)
    for stop_index in range(STOPS + 1):
        if stop_index > 0:
            current = from_behind(current, "blk", 1)
        weight = from_root(screened[0], "blk", stop_index)
        permuted = jnp.take(current, umklapp_map[stop_index], axis=3)
        d_re, d_im = direct_fold(wavefunc, permuted, weight)
        e_re = e_re + d_re
        e_im = e_im + d_im
    direct = finish_direct(wavefunc, e_re, e_im) * scale_direct
    return lax.psum(direct, "pair") + exchange


def solution(mesh):
    placed = (
        P(("grp", "blk"), None, None, None),
        P(("grp", "blk"), None),
        P(("grp", "blk"), None, None),
        P("grp"),
        P(),
    )
    body = eight_blocks if mesh.shape["blk"] == BLOCKS and mesh.shape["pair"] == 2 else any_blocks
    return jax.shard_map(body, mesh=mesh, in_specs=placed, out_specs=P(("grp", "blk"), None), check_vma=False)
```

```python
import functools
import math

import jax
import jax.numpy as jnp
from jax import lax
from jax.experimental import pallas as pl
from jax.experimental.pallas import tpu as pltpu
from jax.sharding import PartitionSpec as P

NV = 8
NC = 8
STOPS = 2
BF = jnp.bfloat16
F32 = jnp.float32

BLOCKS = 8
OFFSET = {0: 0, 4: 0, 1: 1, 5: 1, 2: 2, 3: 2}
TARGETS = {
    (0, 0): (0, 1), (0, 1): (2, 3),
    (1, 0): (1, 0), (1, 1): (3, 2),
    (2, 0): (2, 0), (2, 1): (6, 4),
    (3, 0): (3, 1), (3, 1): (7, 5),
    (4, 0): (4, 5), (4, 1): (7, 6),
    (5, 0): (5, 4), (5, 1): (6, 7),
}
MATRIX_MOVES = ((0, 4), (1, 5), (2, 3))
FETCH = {
    (0, 0): (3, 2), (0, 1): (1, 2),
    (1, 0): (0, 7), (1, 1): (2, 3),
    (2, 0): (0, None), (2, 1): (6, 4),
    (3, 0): (1, None), (3, 1): (7, 5),
    (4, 0): (5, 6), (4, 1): (7, 6),
    (5, 0): (3, 4), (5, 1): (6, 7),
}
SUMS = ((0, 4), (4, 0))


def pick_cores(pairs, fixed):
    taken, out = {}, []
    for src, dst in pairs:
        chip, core = (src, dst[1]) if fixed == "dst" else (dst, src[1])
        used = taken.setdefault(chip, set())
        core = core if core not in used else 1 - core
        assert core not in used
        used.add(core)
        a, b = ((chip, core), dst) if fixed == "dst" else (src, (chip, core))
        out.append((a[0] * 2 + a[1], b[0] * 2 + b[1]))
    return out


def plan():
    fetch = [pick_cores([(got[r], at) for at, got in FETCH.items() if got[r] is not None], "dst") for r in range(2)]
    home = [
        pick_cores([(at, t[1] if at[1] == 0 else t[0]) for at, t in TARGETS.items()], "src"),
        pick_cores([(at, t[1]) for at, t in TARGETS.items() if at[1] == 1], "src"),
    ]
    table = {}
    for chip, core in TARGETS:
        first, second = FETCH[chip, core]
        held = [chip, first, FETCH[chip, 1 - core][0], second]
        off = OFFSET[chip]
        moved = int(any(d == chip for _, d in MATRIX_MOVES))
        row = [1, off, moved, int(off == 0)]
        row += [held.index(t) for t in TARGETS[chip, core]]
        row += [held.index((t - off) % BLOCKS) for t in TARGETS[chip, core]]
        table[chip, core] = row
    return fetch, home, table


FETCH_ROUNDS, HOME_ROUNDS, TABLE = plan()


def entry(who, column):
    value = jnp.int32(0)
    for b in range(BLOCKS):
        if (b, 0) in TABLE and (TABLE[b, 0][column] or TABLE[b, 1][column]):
            here = jnp.where(who[1] == 0, TABLE[b, 0][column], TABLE[b, 1][column])
            value = jnp.where(who[0] == b, here, value)
    return value


def iota(shape, dim):
    return lax.broadcasted_iota(jnp.int32, shape, dim)


def one(cond, sign=None):
    hit = jnp.where(cond, 1.0, 0.0)
    return hit if sign is None else hit * sign


def dot(a, b, dims=((1,), (0,)), **kw):
    return lax.dot_general(a, b, (dims, ((), ())), preferred_element_type=F32, **kw)


def message_kernel(flat, hay, mine, again):
    rows, planes = flat.shape
    kr = hay.shape[0]
    mine[0:rows, :] = flat[...]
    h = hay[...]
    hi = h.astype(BF)
    lo = (h - hi.astype(F32)).astype(BF)
    both = jnp.concatenate([hi.astype(F32), lo.astype(F32)], axis=1)
    mine[rows : rows + 16, :] = jnp.zeros((16, planes), BF)
    mine[rows : rows + 16, 0:256] = jnp.concatenate([both, jnp.zeros((16 - kr, 256), F32)], axis=0).astype(BF)
    again[0 : rows + 16, :] = mine[...]
    again[rows + 16 :, :] = jnp.zeros((again.shape[0] - rows - 16, planes), BF)


def perm_kernel(who, umk, perm):
    planes = perm.shape[0]
    row = umk[pl.ds(entry(who, 1), 1), :]
    perm[...] = one(iota((planes, planes), 0) == row).astype(BF)


def amplitude(msg, v, c):
    rows = v.shape[0]
    for k in range(rows // 16):
        v[16 * k : 16 * k + 16, :] = msg[32 * k : 32 * k + 16, :]
        c[16 * k : 16 * k + 16, :] = msg[32 * k + 16 : 32 * k + 32, :]
    spread = one(iota((rows, 16), 1) == iota((rows, 16), 0) // 16).astype(BF)
    keep = (iota((rows, 256), 1) % 8) == ((iota((rows, 256), 0) // 2) % 8)
    a = iota((128, rows), 0)
    b = iota((128, rows), 1)
    same_v = ((a // 8) % 8) == ((b // 2) % 8)
    part_a, part_b = a // 64, b % 2
    q0 = one(same_v & (part_a == part_b), jnp.where(part_a == 1, -1.0, 1.0))
    q1 = one(same_v & (part_a != part_b))
    q = jnp.concatenate([q0, q1], axis=1).astype(BF)
    block = (iota((rows, rows), 0) // 16) == (iota((rows, rows), 1) // 16)
    real_row = (iota((rows, rows), 0) % 2) == 0
    x = jnp.where(keep, dot(spread, msg[2 * rows : 2 * rows + 16, 0:256]), 0.0).astype(BF)
    pieces = []
    for piece in (x[:, 0:128], x[:, 128:256]):
        y = dot(piece, q)
        y0, y1 = y[:, :rows], y[:, rows:]
        pieces.append(jnp.where(block, jnp.where(real_row, y0, y1), 0.0).astype(BF))
        pieces.append(jnp.where(block, jnp.where(real_row, y1, -y0), 0.0).astype(BF))
    bands = v[...]
    return dot(pieces[0], bands) + dot(pieces[2], bands), dot(pieces[1], bands) + dot(pieces[3], bands)


def sums(c, amp, turned):
    cf = c[...].astype(F32)
    return jnp.concatenate([jnp.sum(cf * amp, axis=0, keepdims=True), jnp.sum(cf * turned, axis=0, keepdims=True)], axis=0)


def turn_matrix(rows):
    rr, cc = iota((rows, rows), 0), iota((rows, rows), 1)
    pairs = one(rr == (cc + 1 - 2 * (cc % 2)))
    return jnp.where(rr % 2 == 0, pairs, -pairs).astype(BF)


def permute(a, c, perm, ap_refs, wt_refs, cb_refs):
    n = len(ap_refs)
    rows = c.shape[0] // n
    turn = turn_matrix(rows)
    wp = dot(c[...], perm[...])
    ap = dot(a[...], perm[...]).astype(BF)
    for j in range(n):
        part = slice(j * rows, (j + 1) * rows)
        ap_refs[j][0:rows, :] = ap[part]
        ap_refs[j][rows : 2 * rows, :] = dot(turn, ap[part]).astype(BF)
        wt_refs[j][...] = jnp.transpose(wp[part]).astype(BF)
        cb_refs[j][...] = (-dot(turn, c[part, :])).astype(BF)


def prep_kernel(n, n_sums, who, perm, *refs):
    msgs, earlier, (ap, wt, v, ca, cb, xs, a_scr) = refs[:n], refs[n : n + n_sums], refs[n + n_sums :]
    rows, planes = v.shape[1:]
    total = jnp.zeros((2, planes), F32)
    for ref in earlier:
        total = total + ref[...]
    for j in range(n):
        mine = pl.ds(j * rows, rows)
        amp, turned = amplitude(msgs[j], v.at[j], ca.at[mine])
        total = total + sums(ca.at[mine], amp, turned)
        a_scr[mine, :] = amp.astype(BF)
    xs[...] = total

    @pl.when(entry(who, 0) == 1)
    def _():
        each = range(n)
        permute(a_scr, ca, perm, [ap.at[j] for j in each], [wt.at[j] for j in each], [cb.at[j] for j in each])


def last_kernel(who, msg, earlier, v, c, a, xs):
    @pl.when(entry(who, 0) == 1)
    def _():
        amp, turned = amplitude(msg, v, c)
        a[...] = amp.astype(BF)
        xs[...] = earlier[...] + sums(c, amp, turned)

    @pl.when(entry(who, 0) == 0)
    def _():
        xs[...] = jnp.zeros_like(xs)


def pick_kernel(who, perm, *refs):
    own, two, (v_3, c_3, a_3) = refs[0:5], refs[5:10], refs[10:13]
    ap_ref, wt_ref, vt_ref, ca_ref, cb_ref, ap_3, wt_3, cb_3 = refs[13:]
    rows = v_3.shape[0]

    @pl.when(entry(who, 0) == 1)
    def _():
        permute(a_3, c_3, perm, [ap_3], [wt_3], [cb_3])

    def held(slot):
        if slot == 3:
            return ap_3, wt_3, v_3, c_3, cb_3
        ap, wt, v, ca, cb = own if slot == 0 else two
        j = max(slot - 1, 0)
        return ap.at[j], wt.at[j], v.at[j], ca.at[pl.ds(j * rows, rows)], cb.at[j]

    for i in range(2):
        for slot in range(4):

            @pl.when((entry(who, 0) == 1) & (entry(who, 4 + i) == slot))
            def _(i=i, slot=slot):
                _, _, v, ca, cb = held(slot)
                vt_ref[i], ca_ref[i], cb_ref[i] = v[...], ca[...], cb[...]

            @pl.when((entry(who, 0) == 1) & (entry(who, 6 + i) == slot))
            def _(i=i, slot=slot):
                ap, wt = held(slot)[:2]
                ap_ref[i], wt_ref[i] = ap[...], wt[...]


def main_kernel(who, w_own, w_in, w_swapped, ap, wt, v, ca, cb, d_ref, wf):
    rows, planes = v.shape[1:]
    gh = planes // 2
    p = who[1]

    @pl.when((entry(who, 0) == 1) & (entry(who, 2) == 0))
    def _():
        wf[...] = w_own[...].astype(F32)

    @pl.when((entry(who, 0) == 1) & (entry(who, 2) == 1))
    def _():
        wf[pl.ds(pl.multiple_of(p * gh, 128), gh), :] = w_in[...].astype(F32)
        wf[pl.ds(pl.multiple_of((1 - p) * gh, 128), gh), :] = w_swapped[...].astype(F32)

    @pl.when(entry(who, 0) == 1)
    def _():
        kernels = []
        for i in range(2):
            for h in range(2):
                w = wf[h * gh : (h + 1) * gh, :]
                left = wt[i, h * gh : (h + 1) * gh, :]
                k_re = (w * dot(left, ap[i, 0:rows, :])).astype(BF)
                k_im = (w * dot(left, ap[i, rows : 2 * rows, :])).astype(BF)
                kernels.append((k_re, k_im))
        sides = []
        for i in range(2):
            y = None
            for h in range(2):
                k_re, k_im = kernels[2 * i + h]
                part = slice(h * gh, (h + 1) * gh)
                z = dot(ca[i, :, part], k_re) + dot(cb[i, :, part], k_im)
                y = z if y is None else y + z
            sides.append(y.astype(BF))
        for i, y in enumerate(sides):
            d_ref[i] = dot(y, v[i], ((1,), (1,)))


def finish_kernel(scale_direct, scale_exchange, who, d_ref, v, ca, cb, *refs):
    xs, xs_in, coulomb, stays, goes_1, goes_2 = refs
    rows = v.shape[1]
    kr = rows // 16
    p = who[1]
    a = iota((rows, 128), 0)
    b = iota((rows, 128), 1)
    same_v = ((a // 2) % 8) == ((b // 8) % 8)
    ra, rb = a % 2, b // 64
    qa = one(same_v & (ra == rb), jnp.where(rb == 1, -1.0, 1.0))
    qb = one(same_v & (ra != rb))
    q = jnp.concatenate([qa, qb], axis=1)
    real_row = (a % 2) == 0
    keep = (b % 8) == ((a // 2) % 8)
    block = (iota((rows, rows), 0) // 16) == (iota((rows, rows), 1) // 16)

    def result(d):
        d = jnp.where(block, d, 0.0)
        z = dot(d, q, precision=lax.Precision.HIGHEST)
        z = jnp.where(keep, jnp.where(real_row, z[:, :128], z[:, 128:]), 0.0)
        return jnp.sum(z.reshape(kr, 16, 128), axis=1)

    def store(one_, two):
        r1, r2 = result(one_), result(two)
        core_0 = p == 0
        stays[...] = jnp.where(core_0, r1, 0.0)
        goes_1[...] = jnp.where(core_0, r2, r1)
        goes_2[...] = jnp.where(core_0, 0.0, r2)

    @pl.when(entry(who, 0) == 0)
    def _():
        for o in (stays, goes_1, goes_2):
            o[...] = jnp.zeros_like(o)

    @pl.when((entry(who, 0) == 1) & (entry(who, 3) == 0))
    def _():
        store(*(d_ref[i] * scale_direct for i in range(2)))

    @pl.when((entry(who, 0) == 1) & (entry(who, 3) == 1))
    def _():
        y = coulomb[...] * (xs[...] + xs_in[...]) * scale_exchange
        both = []
        for i in range(2):
            side = (ca[i].astype(F32) * y[0:1] + cb[i].astype(F32) * y[1:2]).astype(BF)
            both.append(d_ref[i] * scale_direct + dot(side, v[i], ((1,), (1,))))
        store(*both)


VM = pl.BlockSpec(memory_space=pltpu.VMEM)
SM = pl.BlockSpec(memory_space=pltpu.SMEM)


def call(kernel, outs, ins, scratch=(), known=True, limit=24 << 20):
    moved = sum(math.prod(x.shape) * x.dtype.itemsize for x in (*ins, *outs)) if known else 0
    specs = [SM if x.dtype == jnp.int32 and x.ndim == 1 else VM for x in ins]
    if not known:
        ins = [x if x.dtype == jnp.int32 else pltpu.with_memory_space_constraint(x, pltpu.VMEM) for x in ins]
        outs = [pltpu.VMEM(x.shape, x.dtype) for x in outs]
    return pl.pallas_call(
        kernel,
        out_shape=outs,
        in_specs=specs,
        out_specs=[VM] * len(outs),
        scratch_shapes=list(scratch),
        compiler_params=pltpu.CompilerParams(vmem_limit_bytes=limit),
        cost_estimate=pl.CostEstimate(flops=0, bytes_accessed=moved, transcendentals=0),
    )(*ins)


PAD = 16


def eight_blocks(wavefunc, haydock, screened, coulomb, umklapp_map):
    kr, nb, _, planes = wavefunc.shape
    rows = kr * 16
    gh = planes // 2
    shape = jax.ShapeDtypeStruct
    member = lax.axis_index("pair").astype(jnp.int32)
    who = jnp.stack([lax.axis_index("blk").astype(jnp.int32), member])

    def over_cores(x, pairs):
        return lax.ppermute(x, ("blk", "pair"), pairs)

    def swap(x):
        return lax.ppermute(x, "pair", [(0, 1), (1, 0)])

    def prep(perm, msgs, earlier=(), known=True):
        n = len(msgs)
        outs = [
            shape((n, 2 * rows, planes), BF),
            shape((n, planes, rows), BF),
            shape((n, rows, planes), BF),
            shape((n * rows, planes), BF),
            shape((n, rows, planes), BF),
            shape((2, planes), F32),
        ]
        return call(
            functools.partial(prep_kernel, n, len(earlier)),
            outs,
            [who, perm, *msgs, *earlier],
            scratch=[pltpu.VMEM((n * rows, planes), BF)],
            known=known,
        )

    w_in = lax.ppermute(lax.dynamic_slice_in_dim(screened[0], member * gh, gh, 0), "blk", MATRIX_MOVES)
    flat = wavefunc.reshape(kr * nb * 2, planes)
    sizes = (2 * rows + 16, 2 * rows + 16 + PAD)
    mine, again = call(message_kernel, [shape((n, planes), BF) for n in sizes], [flat, haydock])
    got_1 = over_cores(mine, FETCH_ROUNDS[0])
    (perm,) = call(perm_kernel, [shape((planes, planes), BF)], [who, umklapp_map])
    own = prep(perm, [mine])
    got_1, *own = lax.optimization_barrier((got_1, *own))
    got_2 = over_cores(again, FETCH_ROUNDS[1])
    two = prep(perm, [got_1, swap(got_1)], [own[5]], known=False)
    got_2, *two = lax.optimization_barrier((got_2, *two))
    bands = shape((rows, planes), BF)
    v_3, c_3, a_3, xs = call(last_kernel, [bands, bands, bands, shape((2, planes), F32)], [who, got_2, two[5]])
    xs_in = lax.ppermute(xs, "blk", SUMS)
    total_k = kr * lax.axis_size("blk")
    scale_exchange = 1.0 / (8.0 * math.sqrt(planes * total_k))
    scale_direct = -1.0 / (8.0 * math.sqrt(planes * kr * (STOPS + 1)))
    item = shape((2, rows, planes), BF)
    ap, wt, v, ca, cb = call(
        pick_kernel,
        [shape((2, 2 * rows, planes), BF), shape((2, planes, rows), BF), item, item, item],
        [who, perm, *own[:5], *two[:5], v_3, c_3, a_3],
        scratch=[
            pltpu.VMEM((2 * rows, planes), BF),
            pltpu.VMEM((planes, rows), BF),
            pltpu.VMEM((rows, planes), BF),
        ],
    )
    w_in, ap, wt = lax.optimization_barrier((w_in, ap, wt))
    (d,) = call(
        main_kernel,
        [shape((2, rows, rows), F32)],
        [who, screened[0], w_in, swap(w_in), ap, wt, v, ca, cb],
        scratch=[pltpu.VMEM((planes, planes), F32)],
    )
    stays, goes_1, goes_2 = call(
        functools.partial(finish_kernel, scale_direct, scale_exchange),
        [shape((kr, 128), F32)] * 3,
        [who, d, v, ca, cb, xs, xs_in, coulomb.reshape(1, planes)],
    )
    total = stays + over_cores(goes_1, HOME_ROUNDS[0]) + over_cores(goes_2, HOME_ROUNDS[1])
    return total + swap(total)


def from_root(block, axis, holder):
    block = jnp.where(lax.axis_index(axis) == holder, block, jnp.zeros_like(block))
    return lax.psum(block, axis)


def from_behind(value, axis, by):
    devices = lax.axis_size(axis)
    return lax.ppermute(value, axis, [(i, (i + by) % devices) for i in range(devices)])


def make_amplitude(wave_rows, amp_rows):
    count = wave_rows.shape[0]
    valence = wave_rows[:, :NV].astype(jnp.float32)
    val_re = valence[:, :, 0]
    val_im = valence[:, :, 1]
    amps = amp_rows.reshape(count, 2, NV, NC)
    amp_re = amps[:, 0]
    amp_im = amps[:, 1]
    out_re = jnp.einsum("kvg,kvc->kcg", val_re, amp_re) - jnp.einsum("kvg,kvc->kcg", val_im, amp_im)
    out_im = jnp.einsum("kvg,kvc->kcg", val_re, amp_im) + jnp.einsum("kvg,kvc->kcg", val_im, amp_re)
    return jnp.stack([out_re, out_im], axis=2).astype(jnp.bfloat16)


def densities(wave_rows):
    wide = wave_rows.astype(jnp.float32)
    val_re = wide[:, :NV, 0][:, :, None, :]
    val_im = wide[:, :NV, 1][:, :, None, :]
    cond_re = wide[:, NV:, 0][:, None, :, :]
    cond_im = wide[:, NV:, 1][:, None, :, :]
    return (val_re * cond_re + val_im * cond_im, val_re * cond_im - val_im * cond_re)


def fold_exchange(dens_re, dens_im, amp_rows):
    count = amp_rows.shape[0]
    amps = amp_rows.reshape(count, 2, NV, NC)
    amp_re = amps[:, 0]
    amp_im = amps[:, 1]
    x_re = jnp.einsum("kvcg,kvc->g", dens_re, amp_re) + jnp.einsum("kvcg,kvc->g", dens_im, amp_im)
    x_im = jnp.einsum("kvcg,kvc->g", dens_re, amp_im) - jnp.einsum("kvcg,kvc->g", dens_im, amp_re)
    return (x_re, x_im)


def exchange_terms(dens_re, dens_im, x_re, x_im, coulomb):
    count = dens_re.shape[0]
    y_re = coulomb * x_re
    y_im = coulomb * x_im
    out_re = jnp.einsum("kvcg,g->kvc", dens_re, y_re) - jnp.einsum("kvcg,g->kvc", dens_im, y_im)
    out_im = jnp.einsum("kvcg,g->kvc", dens_re, y_im) + jnp.einsum("kvcg,g->kvc", dens_im, y_re)
    return jnp.stack([out_re, out_im], axis=1).reshape(count, -1)


def direct_fold(wave_rows, permuted, weight):
    valence = wave_rows[:, :NV].astype(jnp.float32)
    val_re = valence[:, :, 0][:, None, :, None, :]
    val_im = valence[:, :, 1][:, None, :, None, :]
    wide = permuted.astype(jnp.float32)
    ahat_re = wide[:, :NC, 0][None, :, None, :, :]
    ahat_im = wide[:, :NC, 1][None, :, None, :, :]
    cond_re = wide[:, NC:, 0]
    cond_im = wide[:, NC:, 1]
    y_re = val_re * ahat_re + val_im * ahat_im
    y_im = val_re * ahat_im - val_im * ahat_re
    stacked = jnp.stack([y_re, y_im], axis=4).astype(jnp.bfloat16)
    flat = stacked.reshape(-1, weight.shape[1])
    image = lax.dot_general(flat, weight, (((1,), (1,)), ((), ())), preferred_element_type=jnp.float32)
    image = image.reshape(stacked.shape)
    z_re = image[:, :, :, :, 0]
    z_im = image[:, :, :, :, 1]
    e_re = jnp.einsum("kjvcg,jcg->kvg", z_re, cond_re) + jnp.einsum("kjvcg,jcg->kvg", z_im, cond_im)
    e_im = jnp.einsum("kjvcg,jcg->kvg", z_im, cond_re) - jnp.einsum("kjvcg,jcg->kvg", z_re, cond_im)
    return (e_re, e_im)


def finish_direct(wave_rows, e_re, e_im):
    count = wave_rows.shape[0]
    cond = wave_rows[:, NV:].astype(jnp.float32)
    cond_re = cond[:, :, 0]
    cond_im = cond[:, :, 1]
    out_re = jnp.einsum("kcg,kvg->kvc", cond_re, e_re) - jnp.einsum("kcg,kvg->kvc", cond_im, e_im)
    out_im = jnp.einsum("kcg,kvg->kvc", cond_re, e_im) + jnp.einsum("kcg,kvg->kvc", cond_im, e_re)
    return jnp.stack([out_re, out_im], axis=1).reshape(count, -1)


def any_blocks(wavefunc, haydock, screened, coulomb, umklapp_map):
    row_count = wavefunc.shape[0]
    plane_count = wavefunc.shape[3]
    share = row_count // lax.axis_size("pair")
    member = lax.axis_index("pair")
    amplitude = make_amplitude(wavefunc, haydock)
    partner = jnp.concatenate([amplitude, wavefunc[:, NV:]], axis=1)
    current = lax.dynamic_slice_in_dim(partner, member * share, share, 0)
    full_re, full_im = densities(wavefunc)
    share_re = lax.dynamic_slice_in_dim(full_re, member * share, share, 0)
    share_im = lax.dynamic_slice_in_dim(full_im, member * share, share, 0)
    hay_share = lax.dynamic_slice_in_dim(haydock, member * share, share, 0)
    x_re, x_im = fold_exchange(share_re, share_im, hay_share)
    x_re, x_im = lax.psum((x_re, x_im), ("blk", "pair"))
    total_k = row_count * lax.axis_size("blk")
    exchange = exchange_terms(full_re, full_im, x_re, x_im, coulomb) * (
        1.0 / (8.0 * math.sqrt(plane_count * total_k))
    )
    scale_direct = -1.0 / (8.0 * math.sqrt(plane_count * row_count * (STOPS + 1)))
    e_re = jnp.zeros((row_count, NV, plane_count), jnp.float32)
    e_im = jnp.zeros((row_count, NV, plane_count), jnp.float32)
    for stop_index in range(STOPS + 1):
        if stop_index > 0:
            current = from_behind(current, "blk", 1)
        weight = from_root(screened[0], "blk", stop_index)
        permuted = jnp.take(current, umklapp_map[stop_index], axis=3)
        d_re, d_im = direct_fold(wavefunc, permuted, weight)
        e_re = e_re + d_re
        e_im = e_im + d_im
    direct = finish_direct(wavefunc, e_re, e_im) * scale_direct
    return lax.psum(direct, "pair") + exchange


def solution(mesh):
    placed = (
        P(("grp", "blk"), None, None, None),
        P(("grp", "blk"), None),
        P(("grp", "blk"), None, None),
        P("grp"),
        P(),
    )
    body = eight_blocks if mesh.shape["blk"] == BLOCKS and mesh.shape["pair"] == 2 else any_blocks
    return jax.shard_map(body, mesh=mesh, in_specs=placed, out_specs=P(("grp", "blk"), None), check_vma=False)
```

```python
import functools
import math

import jax
import jax.numpy as jnp
from jax import lax
from jax.experimental import pallas as pl
from jax.experimental.pallas import tpu as pltpu
from jax.sharding import PartitionSpec as P

NV = 8
NC = 8
STOPS = 2
BF = jnp.bfloat16
F32 = jnp.float32

BLOCKS = 8
OFFSET = {0: 0, 4: 0, 1: 1, 5: 1, 2: 2, 3: 2}
TARGETS = {
    (0, 0): (0, 1), (0, 1): (2, 3),
    (1, 0): (1, 0), (1, 1): (3, 2),
    (2, 0): (2, 0), (2, 1): (6, 4),
    (3, 0): (3, 1), (3, 1): (7, 5),
    (4, 0): (4, 5), (4, 1): (7, 6),
    (5, 0): (5, 4), (5, 1): (6, 7),
}
MATRIX_MOVES = ((0, 4), (1, 5), (2, 3))
FETCH = {
    (0, 0): (3, 2), (0, 1): (1, 2),
    (1, 0): (0, 7), (1, 1): (2, 3),
    (2, 0): (0, None), (2, 1): (6, 4),
    (3, 0): (1, None), (3, 1): (7, 5),
    (4, 0): (5, 6), (4, 1): (7, 6),
    (5, 0): (3, 4), (5, 1): (6, 7),
}
SUMS = ((0, 4), (4, 0))


def pick_cores(pairs, fixed):
    taken, out = {}, []
    for src, dst in pairs:
        chip, core = (src, dst[1]) if fixed == "dst" else (dst, src[1])
        used = taken.setdefault(chip, set())
        core = core if core not in used else 1 - core
        assert core not in used
        used.add(core)
        a, b = ((chip, core), dst) if fixed == "dst" else (src, (chip, core))
        out.append((a[0] * 2 + a[1], b[0] * 2 + b[1]))
    return out


def plan():
    fetch = [pick_cores([(got[r], at) for at, got in FETCH.items() if got[r] is not None], "dst") for r in range(2)]
    home = [
        pick_cores([(at, t[1] if at[1] == 0 else t[0]) for at, t in TARGETS.items()], "src"),
        pick_cores([(at, t[1]) for at, t in TARGETS.items() if at[1] == 1], "src"),
    ]
    table = {}
    for chip, core in TARGETS:
        first, second = FETCH[chip, core]
        held = [chip, first, FETCH[chip, 1 - core][0], second]
        off = OFFSET[chip]
        moved = int(any(d == chip for _, d in MATRIX_MOVES))
        row = [1, off, moved, int(off == 0)]
        row += [held.index(t) for t in TARGETS[chip, core]]
        row += [held.index((t - off) % BLOCKS) for t in TARGETS[chip, core]]
        table[chip, core] = row
    return fetch, home, table


FETCH_ROUNDS, HOME_ROUNDS, TABLE = plan()


def entry(who, column):
    value = jnp.int32(0)
    for b in range(BLOCKS):
        if (b, 0) in TABLE and (TABLE[b, 0][column] or TABLE[b, 1][column]):
            here = jnp.where(who[1] == 0, TABLE[b, 0][column], TABLE[b, 1][column])
            value = jnp.where(who[0] == b, here, value)
    return value


def iota(shape, dim):
    return lax.broadcasted_iota(jnp.int32, shape, dim)


def one(cond, sign=None):
    hit = jnp.where(cond, 1.0, 0.0)
    return hit if sign is None else hit * sign


def dot(a, b, dims=((1,), (0,)), **kw):
    return lax.dot_general(a, b, (dims, ((), ())), preferred_element_type=F32, **kw)


def message_kernel(flat, hay, mine, again):
    rows, planes = flat.shape
    kr = hay.shape[0]
    mine[0:rows, :] = flat[...]
    h = hay[...]
    hi = h.astype(BF)
    lo = (h - hi.astype(F32)).astype(BF)
    both = jnp.concatenate([hi.astype(F32), lo.astype(F32)], axis=1)
    mine[rows : rows + 16, :] = jnp.zeros((16, planes), BF)
    mine[rows : rows + 16, 0:256] = jnp.concatenate([both, jnp.zeros((16 - kr, 256), F32)], axis=0).astype(BF)
    again[0 : rows + 16, :] = mine[...]
    again[rows + 16 :, :] = jnp.zeros((again.shape[0] - rows - 16, planes), BF)


def perm_kernel(who, umk, perm):
    planes = perm.shape[0]
    row = umk[pl.ds(entry(who, 1), 1), :]
    perm[...] = one(iota((planes, planes), 0) == row).astype(BF)


def amplitude(msg, v, c):
    rows = v.shape[0]
    for k in range(rows // 16):
        v[16 * k : 16 * k + 16, :] = msg[32 * k : 32 * k + 16, :]
        c[16 * k : 16 * k + 16, :] = msg[32 * k + 16 : 32 * k + 32, :]
    spread = one(iota((rows, 16), 1) == iota((rows, 16), 0) // 16).astype(BF)
    keep = (iota((rows, 256), 1) % 8) == ((iota((rows, 256), 0) // 2) % 8)
    a = iota((128, rows), 0)
    b = iota((128, rows), 1)
    same_v = ((a // 8) % 8) == ((b // 2) % 8)
    part_a, part_b = a // 64, b % 2
    q0 = one(same_v & (part_a == part_b), jnp.where(part_a == 1, -1.0, 1.0))
    q1 = one(same_v & (part_a != part_b))
    q = jnp.concatenate([q0, q1], axis=1).astype(BF)
    block = (iota((rows, rows), 0) // 16) == (iota((rows, rows), 1) // 16)
    real_row = (iota((rows, rows), 0) % 2) == 0
    x = jnp.where(keep, dot(spread, msg[2 * rows : 2 * rows + 16, 0:256]), 0.0).astype(BF)
    pieces = []
    for piece in (x[:, 0:128], x[:, 128:256]):
        y = dot(piece, q)
        y0, y1 = y[:, :rows], y[:, rows:]
        pieces.append(jnp.where(block, jnp.where(real_row, y0, y1), 0.0).astype(BF))
        pieces.append(jnp.where(block, jnp.where(real_row, y1, -y0), 0.0).astype(BF))
    bands = v[...]
    return dot(pieces[0], bands) + dot(pieces[2], bands), dot(pieces[1], bands) + dot(pieces[3], bands)


def sums(c, amp, turned):
    cf = c[...].astype(F32)
    return jnp.concatenate([jnp.sum(cf * amp, axis=0, keepdims=True), jnp.sum(cf * turned, axis=0, keepdims=True)], axis=0)


def turn_matrix(rows):
    rr, cc = iota((rows, rows), 0), iota((rows, rows), 1)
    pairs = one(rr == (cc + 1 - 2 * (cc % 2)))
    return jnp.where(rr % 2 == 0, pairs, -pairs).astype(BF)


def permute(a, c, perm, ap_refs, wt_refs, cb_refs):
    n = len(ap_refs)
    rows = c.shape[0] // n
    turn = turn_matrix(rows)
    wp = dot(c[...], perm[...])
    ap = dot(a[...], perm[...]).astype(BF)
    for j in range(n):
        part = slice(j * rows, (j + 1) * rows)
        ap_refs[j][0:rows, :] = ap[part]
        ap_refs[j][rows : 2 * rows, :] = dot(turn, ap[part]).astype(BF)
        wt_refs[j][...] = jnp.transpose(wp[part]).astype(BF)
        cb_refs[j][...] = (-dot(turn, c[part, :])).astype(BF)


def prep_kernel(n, n_sums, who, perm, *refs):
    msgs, earlier, (ap, wt, v, ca, cb, xs, a_scr) = refs[:n], refs[n : n + n_sums], refs[n + n_sums :]
    rows, planes = v.shape[1:]
    total = jnp.zeros((2, planes), F32)
    for ref in earlier:
        total = total + ref[...]
    for j in range(n):
        mine = pl.ds(j * rows, rows)
        amp, turned = amplitude(msgs[j], v.at[j], ca.at[mine])
        total = total + sums(ca.at[mine], amp, turned)
        a_scr[mine, :] = amp.astype(BF)
    xs[...] = total

    @pl.when(entry(who, 0) == 1)
    def _():
        each = range(n)
        permute(a_scr, ca, perm, [ap.at[j] for j in each], [wt.at[j] for j in each], [cb.at[j] for j in each])


def pick_kernel(who, perm, msg, earlier, *refs):
    own, two = refs[0:5], refs[5:10]
    ap_ref, wt_ref, vt_ref, ca_ref, cb_ref, xs, ap_3, wt_3, v_3, c_3, cb_3, a_3 = refs[10:]
    rows = v_3.shape[0]

    @pl.when(entry(who, 0) == 1)
    def _():
        amp, turned = amplitude(msg, v_3, c_3)
        a_3[...] = amp.astype(BF)
        xs[...] = earlier[...] + sums(c_3, amp, turned)
        permute(a_3, c_3, perm, [ap_3], [wt_3], [cb_3])

    @pl.when(entry(who, 0) == 0)
    def _():
        xs[...] = jnp.zeros_like(xs)

    def held(slot):
        if slot == 3:
            return ap_3, wt_3, v_3, c_3, cb_3
        ap, wt, v, ca, cb = own if slot == 0 else two
        j = max(slot - 1, 0)
        return ap.at[j], wt.at[j], v.at[j], ca.at[pl.ds(j * rows, rows)], cb.at[j]

    for i in range(2):
        for slot in range(4):

            @pl.when((entry(who, 0) == 1) & (entry(who, 4 + i) == slot))
            def _(i=i, slot=slot):
                _, _, v, ca, cb = held(slot)
                vt_ref[i], ca_ref[i], cb_ref[i] = v[...], ca[...], cb[...]

            @pl.when((entry(who, 0) == 1) & (entry(who, 6 + i) == slot))
            def _(i=i, slot=slot):
                ap, wt = held(slot)[:2]
                ap_ref[i], wt_ref[i] = ap[...], wt[...]


def main_kernel(who, w_own, w_in, w_swapped, ap, wt, v, ca, cb, d_ref, wf):
    rows, planes = v.shape[1:]
    gh = planes // 2
    p = who[1]

    @pl.when((entry(who, 0) == 1) & (entry(who, 2) == 0))
    def _():
        wf[...] = w_own[...].astype(F32)

    @pl.when((entry(who, 0) == 1) & (entry(who, 2) == 1))
    def _():
        wf[pl.ds(pl.multiple_of(p * gh, 128), gh), :] = w_in[...].astype(F32)
        wf[pl.ds(pl.multiple_of((1 - p) * gh, 128), gh), :] = w_swapped[...].astype(F32)

    @pl.when(entry(who, 0) == 1)
    def _():
        kernels = []
        for i in range(2):
            for h in range(2):
                w = wf[h * gh : (h + 1) * gh, :]
                left = wt[i, h * gh : (h + 1) * gh, :]
                k_re = (w * dot(left, ap[i, 0:rows, :])).astype(BF)
                k_im = (w * dot(left, ap[i, rows : 2 * rows, :])).astype(BF)
                kernels.append((k_re, k_im))
        sides = []
        for i in range(2):
            y = None
            for h in range(2):
                k_re, k_im = kernels[2 * i + h]
                part = slice(h * gh, (h + 1) * gh)
                z = dot(ca[i, :, part], k_re) + dot(cb[i, :, part], k_im)
                y = z if y is None else y + z
            sides.append(y.astype(BF))
        for i, y in enumerate(sides):
            d_ref[i] = dot(y, v[i], ((1,), (1,)))


def finish_kernel(scale_direct, scale_exchange, who, d_ref, v, ca, cb, *refs):
    xs, xs_in, coulomb, stays, goes_1, goes_2 = refs
    rows = v.shape[1]
    kr = rows // 16
    p = who[1]
    a = iota((rows, 128), 0)
    b = iota((rows, 128), 1)
    same_v = ((a // 2) % 8) == ((b // 8) % 8)
    ra, rb = a % 2, b // 64
    qa = one(same_v & (ra == rb), jnp.where(rb == 1, -1.0, 1.0))
    qb = one(same_v & (ra != rb))
    q = jnp.concatenate([qa, qb], axis=1)
    real_row = (a % 2) == 0
    keep = (b % 8) == ((a // 2) % 8)
    block = (iota((rows, rows), 0) // 16) == (iota((rows, rows), 1) // 16)

    def result(d):
        d = jnp.where(block, d, 0.0)
        z = dot(d, q, precision=lax.Precision.HIGHEST)
        z = jnp.where(keep, jnp.where(real_row, z[:, :128], z[:, 128:]), 0.0)
        return jnp.sum(z.reshape(kr, 16, 128), axis=1)

    def store(one_, two):
        r1, r2 = result(one_), result(two)
        core_0 = p == 0
        stays[...] = jnp.where(core_0, r1, 0.0)
        goes_1[...] = jnp.where(core_0, r2, r1)
        goes_2[...] = jnp.where(core_0, 0.0, r2)

    @pl.when(entry(who, 0) == 0)
    def _():
        for o in (stays, goes_1, goes_2):
            o[...] = jnp.zeros_like(o)

    @pl.when((entry(who, 0) == 1) & (entry(who, 3) == 0))
    def _():
        store(*(d_ref[i] * scale_direct for i in range(2)))

    @pl.when((entry(who, 0) == 1) & (entry(who, 3) == 1))
    def _():
        y = coulomb[...] * (xs[...] + xs_in[...]) * scale_exchange
        both = []
        for i in range(2):
            side = (ca[i].astype(F32) * y[0:1] + cb[i].astype(F32) * y[1:2]).astype(BF)
            both.append(d_ref[i] * scale_direct + dot(side, v[i], ((1,), (1,))))
        store(*both)


VM = pl.BlockSpec(memory_space=pltpu.VMEM)
SM = pl.BlockSpec(memory_space=pltpu.SMEM)


def call(kernel, outs, ins, scratch=(), known=True, limit=24 << 20):
    moved = sum(math.prod(x.shape) * x.dtype.itemsize for x in (*ins, *outs)) if known else 0
    specs = [SM if x.dtype == jnp.int32 and x.ndim == 1 else VM for x in ins]
    if not known:
        ins = [x if x.dtype == jnp.int32 else pltpu.with_memory_space_constraint(x, pltpu.VMEM) for x in ins]
        outs = [pltpu.VMEM(x.shape, x.dtype) for x in outs]
    return pl.pallas_call(
        kernel,
        out_shape=outs,
        in_specs=specs,
        out_specs=[VM] * len(outs),
        scratch_shapes=list(scratch),
        compiler_params=pltpu.CompilerParams(vmem_limit_bytes=limit),
        cost_estimate=pl.CostEstimate(flops=0, bytes_accessed=moved, transcendentals=0),
    )(*ins)


PAD = 16


def eight_blocks(wavefunc, haydock, screened, coulomb, umklapp_map):
    kr, nb, _, planes = wavefunc.shape
    rows = kr * 16
    gh = planes // 2
    shape = jax.ShapeDtypeStruct
    member = lax.axis_index("pair").astype(jnp.int32)
    who = jnp.stack([lax.axis_index("blk").astype(jnp.int32), member])

    def over_cores(x, pairs):
        return lax.ppermute(x, ("blk", "pair"), pairs)

    def swap(x):
        return lax.ppermute(x, "pair", [(0, 1), (1, 0)])

    def prep(perm, msgs, earlier=(), known=True):
        n = len(msgs)
        outs = [
            shape((n, 2 * rows, planes), BF),
            shape((n, planes, rows), BF),
            shape((n, rows, planes), BF),
            shape((n * rows, planes), BF),
            shape((n, rows, planes), BF),
            shape((2, planes), F32),
        ]
        return call(
            functools.partial(prep_kernel, n, len(earlier)),
            outs,
            [who, perm, *msgs, *earlier],
            scratch=[pltpu.VMEM((n * rows, planes), BF)],
            known=known,
        )

    w_in = lax.ppermute(lax.dynamic_slice_in_dim(screened[0], member * gh, gh, 0), "blk", MATRIX_MOVES)
    flat = wavefunc.reshape(kr * nb * 2, planes)
    sizes = (2 * rows + 16, 2 * rows + 16 + PAD)
    mine, again = call(message_kernel, [shape((n, planes), BF) for n in sizes], [flat, haydock])
    got_1 = over_cores(mine, FETCH_ROUNDS[0])
    (perm,) = call(perm_kernel, [shape((planes, planes), BF)], [who, umklapp_map])
    own = prep(perm, [mine])
    got_1, *own = lax.optimization_barrier((got_1, *own))
    got_2 = over_cores(again, FETCH_ROUNDS[1])
    two = prep(perm, [got_1, swap(got_1)], [own[5]], known=False)
    got_2, *two = lax.optimization_barrier((got_2, *two))
    total_k = kr * lax.axis_size("blk")
    scale_exchange = 1.0 / (8.0 * math.sqrt(planes * total_k))
    scale_direct = -1.0 / (8.0 * math.sqrt(planes * kr * (STOPS + 1)))
    item = shape((2, rows, planes), BF)
    bands = pltpu.VMEM((rows, planes), BF)
    ap, wt, v, ca, cb, xs = call(
        pick_kernel,
        [shape((2, 2 * rows, planes), BF), shape((2, planes, rows), BF), item, item, item, shape((2, planes), F32)],
        [who, perm, got_2, two[5], *own[:5], *two[:5]],
        scratch=[pltpu.VMEM((2 * rows, planes), BF), pltpu.VMEM((planes, rows), BF), bands, bands, bands, bands],
    )
    xs_in = lax.ppermute(xs, "blk", SUMS)
    w_in, ap, wt = lax.optimization_barrier((w_in, ap, wt))
    (d,) = call(
        main_kernel,
        [shape((2, rows, rows), F32)],
        [who, screened[0], w_in, swap(w_in), ap, wt, v, ca, cb],
        scratch=[pltpu.VMEM((planes, planes), F32)],
    )
    stays, goes_1, goes_2 = call(
        functools.partial(finish_kernel, scale_direct, scale_exchange),
        [shape((kr, 128), F32)] * 3,
        [who, d, v, ca, cb, xs, xs_in, coulomb.reshape(1, planes)],
    )
    total = stays + over_cores(goes_1, HOME_ROUNDS[0]) + over_cores(goes_2, HOME_ROUNDS[1])
    return total + swap(total)


def from_root(block, axis, holder):
    block = jnp.where(lax.axis_index(axis) == holder, block, jnp.zeros_like(block))
    return lax.psum(block, axis)


def from_behind(value, axis, by):
    devices = lax.axis_size(axis)
    return lax.ppermute(value, axis, [(i, (i + by) % devices) for i in range(devices)])


def make_amplitude(wave_rows, amp_rows):
    count = wave_rows.shape[0]
    valence = wave_rows[:, :NV].astype(jnp.float32)
    val_re = valence[:, :, 0]
    val_im = valence[:, :, 1]
    amps = amp_rows.reshape(count, 2, NV, NC)
    amp_re = amps[:, 0]
    amp_im = amps[:, 1]
    out_re = jnp.einsum("kvg,kvc->kcg", val_re, amp_re) - jnp.einsum("kvg,kvc->kcg", val_im, amp_im)
    out_im = jnp.einsum("kvg,kvc->kcg", val_re, amp_im) + jnp.einsum("kvg,kvc->kcg", val_im, amp_re)
    return jnp.stack([out_re, out_im], axis=2).astype(jnp.bfloat16)


def densities(wave_rows):
    wide = wave_rows.astype(jnp.float32)
    val_re = wide[:, :NV, 0][:, :, None, :]
    val_im = wide[:, :NV, 1][:, :, None, :]
    cond_re = wide[:, NV:, 0][:, None, :, :]
    cond_im = wide[:, NV:, 1][:, None, :, :]
    return (val_re * cond_re + val_im * cond_im, val_re * cond_im - val_im * cond_re)


def fold_exchange(dens_re, dens_im, amp_rows):
    count = amp_rows.shape[0]
    amps = amp_rows.reshape(count, 2, NV, NC)
    amp_re = amps[:, 0]
    amp_im = amps[:, 1]
    x_re = jnp.einsum("kvcg,kvc->g", dens_re, amp_re) + jnp.einsum("kvcg,kvc->g", dens_im, amp_im)
    x_im = jnp.einsum("kvcg,kvc->g", dens_re, amp_im) - jnp.einsum("kvcg,kvc->g", dens_im, amp_re)
    return (x_re, x_im)


def exchange_terms(dens_re, dens_im, x_re, x_im, coulomb):
    count = dens_re.shape[0]
    y_re = coulomb * x_re
    y_im = coulomb * x_im
    out_re = jnp.einsum("kvcg,g->kvc", dens_re, y_re) - jnp.einsum("kvcg,g->kvc", dens_im, y_im)
    out_im = jnp.einsum("kvcg,g->kvc", dens_re, y_im) + jnp.einsum("kvcg,g->kvc", dens_im, y_re)
    return jnp.stack([out_re, out_im], axis=1).reshape(count, -1)


def direct_fold(wave_rows, permuted, weight):
    valence = wave_rows[:, :NV].astype(jnp.float32)
    val_re = valence[:, :, 0][:, None, :, None, :]
    val_im = valence[:, :, 1][:, None, :, None, :]
    wide = permuted.astype(jnp.float32)
    ahat_re = wide[:, :NC, 0][None, :, None, :, :]
    ahat_im = wide[:, :NC, 1][None, :, None, :, :]
    cond_re = wide[:, NC:, 0]
    cond_im = wide[:, NC:, 1]
    y_re = val_re * ahat_re + val_im * ahat_im
    y_im = val_re * ahat_im - val_im * ahat_re
    stacked = jnp.stack([y_re, y_im], axis=4).astype(jnp.bfloat16)
    flat = stacked.reshape(-1, weight.shape[1])
    image = lax.dot_general(flat, weight, (((1,), (1,)), ((), ())), preferred_element_type=jnp.float32)
    image = image.reshape(stacked.shape)
    z_re = image[:, :, :, :, 0]
    z_im = image[:, :, :, :, 1]
    e_re = jnp.einsum("kjvcg,jcg->kvg", z_re, cond_re) + jnp.einsum("kjvcg,jcg->kvg", z_im, cond_im)
    e_im = jnp.einsum("kjvcg,jcg->kvg", z_im, cond_re) - jnp.einsum("kjvcg,jcg->kvg", z_re, cond_im)
    return (e_re, e_im)


def finish_direct(wave_rows, e_re, e_im):
    count = wave_rows.shape[0]
    cond = wave_rows[:, NV:].astype(jnp.float32)
    cond_re = cond[:, :, 0]
    cond_im = cond[:, :, 1]
    out_re = jnp.einsum("kcg,kvg->kvc", cond_re, e_re) - jnp.einsum("kcg,kvg->kvc", cond_im, e_im)
    out_im = jnp.einsum("kcg,kvg->kvc", cond_re, e_im) + jnp.einsum("kcg,kvg->kvc", cond_im, e_re)
    return jnp.stack([out_re, out_im], axis=1).reshape(count, -1)


def any_blocks(wavefunc, haydock, screened, coulomb, umklapp_map):
    row_count = wavefunc.shape[0]
    plane_count = wavefunc.shape[3]
    share = row_count // lax.axis_size("pair")
    member = lax.axis_index("pair")
    amplitude = make_amplitude(wavefunc, haydock)
    partner = jnp.concatenate([amplitude, wavefunc[:, NV:]], axis=1)
    current = lax.dynamic_slice_in_dim(partner, member * share, share, 0)
    full_re, full_im = densities(wavefunc)
    share_re = lax.dynamic_slice_in_dim(full_re, member * share, share, 0)
    share_im = lax.dynamic_slice_in_dim(full_im, member * share, share, 0)
    hay_share = lax.dynamic_slice_in_dim(haydock, member * share, share, 0)
    x_re, x_im = fold_exchange(share_re, share_im, hay_share)
    x_re, x_im = lax.psum((x_re, x_im), ("blk", "pair"))
    total_k = row_count * lax.axis_size("blk")
    exchange = exchange_terms(full_re, full_im, x_re, x_im, coulomb) * (
        1.0 / (8.0 * math.sqrt(plane_count * total_k))
    )
    scale_direct = -1.0 / (8.0 * math.sqrt(plane_count * row_count * (STOPS + 1)))
    e_re = jnp.zeros((row_count, NV, plane_count), jnp.float32)
    e_im = jnp.zeros((row_count, NV, plane_count), jnp.float32)
    for stop_index in range(STOPS + 1):
        if stop_index > 0:
            current = from_behind(current, "blk", 1)
        weight = from_root(screened[0], "blk", stop_index)
        permuted = jnp.take(current, umklapp_map[stop_index], axis=3)
        d_re, d_im = direct_fold(wavefunc, permuted, weight)
        e_re = e_re + d_re
        e_im = e_im + d_im
    direct = finish_direct(wavefunc, e_re, e_im) * scale_direct
    return lax.psum(direct, "pair") + exchange


def solution(mesh):
    placed = (
        P(("grp", "blk"), None, None, None),
        P(("grp", "blk"), None),
        P(("grp", "blk"), None, None),
        P("grp"),
        P(),
    )
    body = eight_blocks if mesh.shape["blk"] == BLOCKS and mesh.shape["pair"] == 2 else any_blocks
    return jax.shard_map(body, mesh=mesh, in_specs=placed, out_specs=P(("grp", "blk"), None), check_vma=False)
```

```python
import functools
import math

import jax
import jax.numpy as jnp
from jax import lax
from jax.experimental import pallas as pl
from jax.experimental.pallas import tpu as pltpu
from jax.sharding import PartitionSpec as P

NV = 8
NC = 8
STOPS = 2
BF = jnp.bfloat16
F32 = jnp.float32

BLOCKS = 8
OFFSET = {0: 0, 4: 0, 1: 1, 5: 1, 2: 2, 3: 2}
TARGETS = {
    (0, 0): (0, 1), (0, 1): (2, 3),
    (1, 0): (1, 0), (1, 1): (3, 2),
    (2, 0): (2, 0), (2, 1): (6, 4),
    (3, 0): (3, 1), (3, 1): (7, 5),
    (4, 0): (4, 5), (4, 1): (7, 6),
    (5, 0): (5, 4), (5, 1): (6, 7),
}
MATRIX_MOVES = ((0, 4), (1, 5), (2, 3))
FETCH = {
    (0, 0): (3, 2), (0, 1): (1, 2),
    (1, 0): (0, 7), (1, 1): (2, 3),
    (2, 0): (0, None), (2, 1): (6, 4),
    (3, 0): (1, None), (3, 1): (7, 5),
    (4, 0): (5, 6), (4, 1): (7, 6),
    (5, 0): (3, 4), (5, 1): (6, 7),
}
SUMS = ((0, 4), (4, 0))


def pick_cores(pairs, fixed):
    taken, out = {}, []
    for src, dst in pairs:
        chip, core = (src, dst[1]) if fixed == "dst" else (dst, src[1])
        used = taken.setdefault(chip, set())
        core = core if core not in used else 1 - core
        assert core not in used
        used.add(core)
        a, b = ((chip, core), dst) if fixed == "dst" else (src, (chip, core))
        out.append((a[0] * 2 + a[1], b[0] * 2 + b[1]))
    return out


def plan():
    fetch = [pick_cores([(got[r], at) for at, got in FETCH.items() if got[r] is not None], "dst") for r in range(2)]
    home = [
        pick_cores([(at, t[1] if at[1] == 0 else t[0]) for at, t in TARGETS.items()], "src"),
        pick_cores([(at, t[1]) for at, t in TARGETS.items() if at[1] == 1], "src"),
    ]
    table = {}
    for chip, core in TARGETS:
        first, second = FETCH[chip, core]
        held = [chip, first, FETCH[chip, 1 - core][0], second]
        off = OFFSET[chip]
        moved = int(any(d == chip for _, d in MATRIX_MOVES))
        row = [1, off, moved, int(off == 0)]
        row += [held.index(t) for t in TARGETS[chip, core]]
        row += [held.index((t - off) % BLOCKS) for t in TARGETS[chip, core]]
        table[chip, core] = row
    return fetch, home, table


FETCH_ROUNDS, HOME_ROUNDS, TABLE = plan()


def entry(who, column):
    value = jnp.int32(0)
    for b in range(BLOCKS):
        if (b, 0) in TABLE and (TABLE[b, 0][column] or TABLE[b, 1][column]):
            here = jnp.where(who[1] == 0, TABLE[b, 0][column], TABLE[b, 1][column])
            value = jnp.where(who[0] == b, here, value)
    return value


def iota(shape, dim):
    return lax.broadcasted_iota(jnp.int32, shape, dim)


def one(cond, sign=None):
    hit = jnp.where(cond, 1.0, 0.0)
    return hit if sign is None else hit * sign


def dot(a, b, dims=((1,), (0,)), **kw):
    return lax.dot_general(a, b, (dims, ((), ())), preferred_element_type=F32, **kw)


def message_kernel(flat, hay, mine, again):
    rows, planes = flat.shape
    kr = hay.shape[0]
    mine[0:rows, :] = flat[...]
    h = hay[...]
    hi = h.astype(BF)
    lo = (h - hi.astype(F32)).astype(BF)
    both = jnp.concatenate([hi.astype(F32), lo.astype(F32)], axis=1)
    mine[rows : rows + 16, :] = jnp.zeros((16, planes), BF)
    mine[rows : rows + 16, 0:256] = jnp.concatenate([both, jnp.zeros((16 - kr, 256), F32)], axis=0).astype(BF)
    again[0 : rows + 16, :] = mine[...]
    again[rows + 16 :, :] = jnp.zeros((again.shape[0] - rows - 16, planes), BF)


def perm_kernel(who, umk, perm):
    planes = perm.shape[0]
    row = umk[pl.ds(entry(who, 1), 1), :]
    perm[...] = one(iota((planes, planes), 0) == row).astype(BF)


def amplitude(msg, v, c):
    rows = v.shape[0]
    for k in range(rows // 16):
        v[16 * k : 16 * k + 16, :] = msg[32 * k : 32 * k + 16, :]
        c[16 * k : 16 * k + 16, :] = msg[32 * k + 16 : 32 * k + 32, :]
    spread = one(iota((rows, 16), 1) == iota((rows, 16), 0) // 16).astype(BF)
    keep = (iota((rows, 256), 1) % 8) == ((iota((rows, 256), 0) // 2) % 8)
    a = iota((128, rows), 0)
    b = iota((128, rows), 1)
    same_v = ((a // 8) % 8) == ((b // 2) % 8)
    part_a, part_b = a // 64, b % 2
    q0 = one(same_v & (part_a == part_b), jnp.where(part_a == 1, -1.0, 1.0))
    q1 = one(same_v & (part_a != part_b))
    q = jnp.concatenate([q0, q1], axis=1).astype(BF)
    block = (iota((rows, rows), 0) // 16) == (iota((rows, rows), 1) // 16)
    real_row = (iota((rows, rows), 0) % 2) == 0
    x = jnp.where(keep, dot(spread, msg[2 * rows : 2 * rows + 16, 0:256]), 0.0).astype(BF)
    pieces = []
    for piece in (x[:, 0:128], x[:, 128:256]):
        y = dot(piece, q)
        y0, y1 = y[:, :rows], y[:, rows:]
        pieces.append(jnp.where(block, jnp.where(real_row, y0, y1), 0.0).astype(BF))
        pieces.append(jnp.where(block, jnp.where(real_row, y1, -y0), 0.0).astype(BF))
    bands = v[...]
    return dot(pieces[0], bands) + dot(pieces[2], bands), dot(pieces[1], bands) + dot(pieces[3], bands)


def sums(c, amp, turned):
    cf = c[...].astype(F32)
    return jnp.concatenate([jnp.sum(cf * amp, axis=0, keepdims=True), jnp.sum(cf * turned, axis=0, keepdims=True)], axis=0)


def turn_matrix(rows):
    rr, cc = iota((rows, rows), 0), iota((rows, rows), 1)
    pairs = one(rr == (cc + 1 - 2 * (cc % 2)))
    return jnp.where(rr % 2 == 0, pairs, -pairs).astype(BF)


def permute(a, c, perm, ap_refs, wt_refs, cb_refs):
    n = len(ap_refs)
    rows = c.shape[0] // n
    turn = turn_matrix(rows)
    wp = dot(c[...], perm[...])
    ap = dot(a[...], perm[...]).astype(BF)
    for j in range(n):
        part = slice(j * rows, (j + 1) * rows)
        ap_refs[j][0:rows, :] = ap[part]
        ap_refs[j][rows : 2 * rows, :] = dot(turn, ap[part]).astype(BF)
        wt_refs[j][...] = jnp.transpose(wp[part]).astype(BF)
        cb_refs[j][...] = (-dot(turn, c[part, :])).astype(BF)


def prep_kernel(n, n_sums, who, perm, *refs):
    msgs, earlier, (ap, wt, v, ca, cb, xs, a_scr) = refs[:n], refs[n : n + n_sums], refs[n + n_sums :]
    rows, planes = v.shape[1:]
    total = jnp.zeros((2, planes), F32)
    for ref in earlier:
        total = total + ref[...]
    for j in range(n):
        mine = pl.ds(j * rows, rows)
        amp, turned = amplitude(msgs[j], v.at[j], ca.at[mine])
        total = total + sums(ca.at[mine], amp, turned)
        a_scr[mine, :] = amp.astype(BF)
    xs[...] = total

    @pl.when(entry(who, 0) == 1)
    def _():
        each = range(n)
        permute(a_scr, ca, perm, [ap.at[j] for j in each], [wt.at[j] for j in each], [cb.at[j] for j in each])


def pick_kernel(who, perm, msg, earlier, *refs):
    own, two = refs[0:5], refs[5:10]
    ap_ref, wt_ref, vt_ref, ca_ref, cb_ref, xs, ap_3, wt_3, v_3, c_3, cb_3, a_3 = refs[10:]
    rows = v_3.shape[0]

    @pl.when(entry(who, 0) == 1)
    def _():
        amp, turned = amplitude(msg, v_3, c_3)
        a_3[...] = amp.astype(BF)
        xs[...] = earlier[...] + sums(c_3, amp, turned)
        permute(a_3, c_3, perm, [ap_3], [wt_3], [cb_3])

    @pl.when(entry(who, 0) == 0)
    def _():
        xs[...] = jnp.zeros_like(xs)

    def held(slot):
        if slot == 3:
            return ap_3, wt_3, v_3, c_3, cb_3
        ap, wt, v, ca, cb = own if slot == 0 else two
        j = max(slot - 1, 0)
        return ap.at[j], wt.at[j], v.at[j], ca.at[pl.ds(j * rows, rows)], cb.at[j]

    for i in range(2):
        for slot in range(4):

            @pl.when((entry(who, 0) == 1) & (entry(who, 4 + i) == slot))
            def _(i=i, slot=slot):
                _, _, v, ca, cb = held(slot)
                vt_ref[i], ca_ref[i], cb_ref[i] = v[...], ca[...], cb[...]

            @pl.when((entry(who, 0) == 1) & (entry(who, 6 + i) == slot))
            def _(i=i, slot=slot):
                ap, wt = held(slot)[:2]
                ap_ref[i], wt_ref[i] = ap[...], wt[...]


def main_kernel(who, w_own, w_in, w_swapped, ap, wt, v, ca, cb, d_ref, wf):
    rows, planes = v.shape[1:]
    gh = planes // 2
    p = who[1]

    @pl.when((entry(who, 0) == 1) & (entry(who, 2) == 0))
    def _():
        wf[...] = w_own[...]

    @pl.when((entry(who, 0) == 1) & (entry(who, 2) == 1))
    def _():
        wf[pl.ds(pl.multiple_of(p * gh, 128), gh), :] = w_in[...]
        wf[pl.ds(pl.multiple_of((1 - p) * gh, 128), gh), :] = w_swapped[...]

    @pl.when(entry(who, 0) == 1)
    def _():
        kernels = []
        for i in range(2):
            for h in range(2):
                w = wf[h * gh : (h + 1) * gh, :].astype(F32)
                left = wt[i, h * gh : (h + 1) * gh, :]
                k_re = (w * dot(left, ap[i, 0:rows, :])).astype(BF)
                k_im = (w * dot(left, ap[i, rows : 2 * rows, :])).astype(BF)
                kernels.append((k_re, k_im))
        sides = []
        for i in range(2):
            y = None
            for h in range(2):
                k_re, k_im = kernels[2 * i + h]
                part = slice(h * gh, (h + 1) * gh)
                z = dot(ca[i, :, part], k_re) + dot(cb[i, :, part], k_im)
                y = z if y is None else y + z
            sides.append(y.astype(BF))
        for i, y in enumerate(sides):
            d_ref[i] = dot(y, v[i], ((1,), (1,)))


def finish_kernel(scale_direct, scale_exchange, who, d_ref, v, ca, cb, *refs):
    xs, xs_in, coulomb, stays, goes_1, goes_2 = refs
    rows = v.shape[1]
    kr = rows // 16
    p = who[1]
    a = iota((rows, 128), 0)
    b = iota((rows, 128), 1)
    same_v = ((a // 2) % 8) == ((b // 8) % 8)
    ra, rb = a % 2, b // 64
    qa = one(same_v & (ra == rb), jnp.where(rb == 1, -1.0, 1.0))
    qb = one(same_v & (ra != rb))
    q = jnp.concatenate([qa, qb], axis=1).astype(BF)
    real_row = (a % 2) == 0
    keep = (b % 8) == ((a // 2) % 8)
    block = (iota((rows, rows), 0) // 16) == (iota((rows, rows), 1) // 16)

    def result(d):
        d = jnp.where(block, d, 0.0)
        hi = d.astype(BF)
        lo = (d - hi.astype(F32)).astype(BF)
        z = dot(hi, q) + dot(lo, q)
        z = jnp.where(keep, jnp.where(real_row, z[:, :128], z[:, 128:]), 0.0)
        return jnp.sum(z.reshape(kr, 16, 128), axis=1)

    def store(one_, two):
        r1, r2 = result(one_), result(two)
        core_0 = p == 0
        stays[...] = jnp.where(core_0, r1, 0.0)
        goes_1[...] = jnp.where(core_0, r2, r1)
        goes_2[...] = jnp.where(core_0, 0.0, r2)

    @pl.when(entry(who, 0) == 0)
    def _():
        for o in (stays, goes_1, goes_2):
            o[...] = jnp.zeros_like(o)

    @pl.when((entry(who, 0) == 1) & (entry(who, 3) == 0))
    def _():
        store(*(d_ref[i] * scale_direct for i in range(2)))

    @pl.when((entry(who, 0) == 1) & (entry(who, 3) == 1))
    def _():
        y = coulomb[...] * (xs[...] + xs_in[...]) * scale_exchange
        both = []
        for i in range(2):
            side = (ca[i].astype(F32) * y[0:1] + cb[i].astype(F32) * y[1:2]).astype(BF)
            both.append(d_ref[i] * scale_direct + dot(side, v[i], ((1,), (1,))))
        store(*both)


VM = pl.BlockSpec(memory_space=pltpu.VMEM)
SM = pl.BlockSpec(memory_space=pltpu.SMEM)


def call(kernel, outs, ins, scratch=(), known=True, limit=24 << 20):
    moved = sum(math.prod(x.shape) * x.dtype.itemsize for x in (*ins, *outs)) if known else 0
    specs = [SM if x.dtype == jnp.int32 and x.ndim == 1 else VM for x in ins]
    if not known:
        ins = [x if x.dtype == jnp.int32 else pltpu.with_memory_space_constraint(x, pltpu.VMEM) for x in ins]
        outs = [pltpu.VMEM(x.shape, x.dtype) for x in outs]
    return pl.pallas_call(
        kernel,
        out_shape=outs,
        in_specs=specs,
        out_specs=[VM] * len(outs),
        scratch_shapes=list(scratch),
        compiler_params=pltpu.CompilerParams(vmem_limit_bytes=limit),
        cost_estimate=pl.CostEstimate(flops=0, bytes_accessed=moved, transcendentals=0),
    )(*ins)


PAD = 16


def eight_blocks(wavefunc, haydock, screened, coulomb, umklapp_map):
    kr, nb, _, planes = wavefunc.shape
    rows = kr * 16
    gh = planes // 2
    shape = jax.ShapeDtypeStruct
    member = lax.axis_index("pair").astype(jnp.int32)
    who = jnp.stack([lax.axis_index("blk").astype(jnp.int32), member])

    def over_cores(x, pairs):
        return lax.ppermute(x, ("blk", "pair"), pairs)

    def swap(x):
        return lax.ppermute(x, "pair", [(0, 1), (1, 0)])

    def prep(perm, msgs, earlier=(), known=True):
        n = len(msgs)
        outs = [
            shape((n, 2 * rows, planes), BF),
            shape((n, planes, rows), BF),
            shape((n, rows, planes), BF),
            shape((n * rows, planes), BF),
            shape((n, rows, planes), BF),
            shape((2, planes), F32),
        ]
        return call(
            functools.partial(prep_kernel, n, len(earlier)),
            outs,
            [who, perm, *msgs, *earlier],
            scratch=[pltpu.VMEM((n * rows, planes), BF)],
            known=known,
        )

    w_in = lax.ppermute(lax.dynamic_slice_in_dim(screened[0], member * gh, gh, 0), "blk", MATRIX_MOVES)
    flat = wavefunc.reshape(kr * nb * 2, planes)
    sizes = (2 * rows + 16, 2 * rows + 16 + PAD)
    mine, again = call(message_kernel, [shape((n, planes), BF) for n in sizes], [flat, haydock])
    got_1 = over_cores(mine, FETCH_ROUNDS[0])
    (perm,) = call(perm_kernel, [shape((planes, planes), BF)], [who, umklapp_map])
    own = prep(perm, [mine])
    got_1, *own = lax.optimization_barrier((got_1, *own))
    got_2 = over_cores(again, FETCH_ROUNDS[1])
    two = prep(perm, [got_1, swap(got_1)], [own[5]], known=False)
    got_2, *two = lax.optimization_barrier((got_2, *two))
    total_k = kr * lax.axis_size("blk")
    scale_exchange = 1.0 / (8.0 * math.sqrt(planes * total_k))
    scale_direct = -1.0 / (8.0 * math.sqrt(planes * kr * (STOPS + 1)))
    item = shape((2, rows, planes), BF)
    bands = pltpu.VMEM((rows, planes), BF)
    ap, wt, v, ca, cb, xs = call(
        pick_kernel,
        [shape((2, 2 * rows, planes), BF), shape((2, planes, rows), BF), item, item, item, shape((2, planes), F32)],
        [who, perm, got_2, two[5], *own[:5], *two[:5]],
        scratch=[pltpu.VMEM((2 * rows, planes), BF), pltpu.VMEM((planes, rows), BF), bands, bands, bands, bands],
    )
    xs_in = lax.ppermute(xs, "blk", SUMS)
    w_in, ap, wt = lax.optimization_barrier((w_in, ap, wt))
    (d,) = call(
        main_kernel,
        [shape((2, rows, rows), F32)],
        [who, screened[0], w_in, swap(w_in), ap, wt, v, ca, cb],
        scratch=[pltpu.VMEM((planes, planes), BF)],
    )
    stays, goes_1, goes_2 = call(
        functools.partial(finish_kernel, scale_direct, scale_exchange),
        [shape((kr, 128), F32)] * 3,
        [who, d, v, ca, cb, xs, xs_in, coulomb.reshape(1, planes)],
    )
    total = stays + over_cores(goes_1, HOME_ROUNDS[0]) + over_cores(goes_2, HOME_ROUNDS[1])
    return total + swap(total)


def from_root(block, axis, holder):
    block = jnp.where(lax.axis_index(axis) == holder, block, jnp.zeros_like(block))
    return lax.psum(block, axis)


def from_behind(value, axis, by):
    devices = lax.axis_size(axis)
    return lax.ppermute(value, axis, [(i, (i + by) % devices) for i in range(devices)])


def make_amplitude(wave_rows, amp_rows):
    count = wave_rows.shape[0]
    valence = wave_rows[:, :NV].astype(jnp.float32)
    val_re = valence[:, :, 0]
    val_im = valence[:, :, 1]
    amps = amp_rows.reshape(count, 2, NV, NC)
    amp_re = amps[:, 0]
    amp_im = amps[:, 1]
    out_re = jnp.einsum("kvg,kvc->kcg", val_re, amp_re) - jnp.einsum("kvg,kvc->kcg", val_im, amp_im)
    out_im = jnp.einsum("kvg,kvc->kcg", val_re, amp_im) + jnp.einsum("kvg,kvc->kcg", val_im, amp_re)
    return jnp.stack([out_re, out_im], axis=2).astype(jnp.bfloat16)


def densities(wave_rows):
    wide = wave_rows.astype(jnp.float32)
    val_re = wide[:, :NV, 0][:, :, None, :]
    val_im = wide[:, :NV, 1][:, :, None, :]
    cond_re = wide[:, NV:, 0][:, None, :, :]
    cond_im = wide[:, NV:, 1][:, None, :, :]
    return (val_re * cond_re + val_im * cond_im, val_re * cond_im - val_im * cond_re)


def fold_exchange(dens_re, dens_im, amp_rows):
    count = amp_rows.shape[0]
    amps = amp_rows.reshape(count, 2, NV, NC)
    amp_re = amps[:, 0]
    amp_im = amps[:, 1]
    x_re = jnp.einsum("kvcg,kvc->g", dens_re, amp_re) + jnp.einsum("kvcg,kvc->g", dens_im, amp_im)
    x_im = jnp.einsum("kvcg,kvc->g", dens_re, amp_im) - jnp.einsum("kvcg,kvc->g", dens_im, amp_re)
    return (x_re, x_im)


def exchange_terms(dens_re, dens_im, x_re, x_im, coulomb):
    count = dens_re.shape[0]
    y_re = coulomb * x_re
    y_im = coulomb * x_im
    out_re = jnp.einsum("kvcg,g->kvc", dens_re, y_re) - jnp.einsum("kvcg,g->kvc", dens_im, y_im)
    out_im = jnp.einsum("kvcg,g->kvc", dens_re, y_im) + jnp.einsum("kvcg,g->kvc", dens_im, y_re)
    return jnp.stack([out_re, out_im], axis=1).reshape(count, -1)


def direct_fold(wave_rows, permuted, weight):
    valence = wave_rows[:, :NV].astype(jnp.float32)
    val_re = valence[:, :, 0][:, None, :, None, :]
    val_im = valence[:, :, 1][:, None, :, None, :]
    wide = permuted.astype(jnp.float32)
    ahat_re = wide[:, :NC, 0][None, :, None, :, :]
    ahat_im = wide[:, :NC, 1][None, :, None, :, :]
    cond_re = wide[:, NC:, 0]
    cond_im = wide[:, NC:, 1]
    y_re = val_re * ahat_re + val_im * ahat_im
    y_im = val_re * ahat_im - val_im * ahat_re
    stacked = jnp.stack([y_re, y_im], axis=4).astype(jnp.bfloat16)
    flat = stacked.reshape(-1, weight.shape[1])
    image = lax.dot_general(flat, weight, (((1,), (1,)), ((), ())), preferred_element_type=jnp.float32)
    image = image.reshape(stacked.shape)
    z_re = image[:, :, :, :, 0]
    z_im = image[:, :, :, :, 1]
    e_re = jnp.einsum("kjvcg,jcg->kvg", z_re, cond_re) + jnp.einsum("kjvcg,jcg->kvg", z_im, cond_im)
    e_im = jnp.einsum("kjvcg,jcg->kvg", z_im, cond_re) - jnp.einsum("kjvcg,jcg->kvg", z_re, cond_im)
    return (e_re, e_im)


def finish_direct(wave_rows, e_re, e_im):
    count = wave_rows.shape[0]
    cond = wave_rows[:, NV:].astype(jnp.float32)
    cond_re = cond[:, :, 0]
    cond_im = cond[:, :, 1]
    out_re = jnp.einsum("kcg,kvg->kvc", cond_re, e_re) - jnp.einsum("kcg,kvg->kvc", cond_im, e_im)
    out_im = jnp.einsum("kcg,kvg->kvc", cond_re, e_im) + jnp.einsum("kcg,kvg->kvc", cond_im, e_re)
    return jnp.stack([out_re, out_im], axis=1).reshape(count, -1)


def any_blocks(wavefunc, haydock, screened, coulomb, umklapp_map):
    row_count = wavefunc.shape[0]
    plane_count = wavefunc.shape[3]
    share = row_count // lax.axis_size("pair")
    member = lax.axis_index("pair")
    amplitude = make_amplitude(wavefunc, haydock)
    partner = jnp.concatenate([amplitude, wavefunc[:, NV:]], axis=1)
    current = lax.dynamic_slice_in_dim(partner, member * share, share, 0)
    full_re, full_im = densities(wavefunc)
    share_re = lax.dynamic_slice_in_dim(full_re, member * share, share, 0)
    share_im = lax.dynamic_slice_in_dim(full_im, member * share, share, 0)
    hay_share = lax.dynamic_slice_in_dim(haydock, member * share, share, 0)
    x_re, x_im = fold_exchange(share_re, share_im, hay_share)
    x_re, x_im = lax.psum((x_re, x_im), ("blk", "pair"))
    total_k = row_count * lax.axis_size("blk")
    exchange = exchange_terms(full_re, full_im, x_re, x_im, coulomb) * (
        1.0 / (8.0 * math.sqrt(plane_count * total_k))
    )
    scale_direct = -1.0 / (8.0 * math.sqrt(plane_count * row_count * (STOPS + 1)))
    e_re = jnp.zeros((row_count, NV, plane_count), jnp.float32)
    e_im = jnp.zeros((row_count, NV, plane_count), jnp.float32)
    for stop_index in range(STOPS + 1):
        if stop_index > 0:
            current = from_behind(current, "blk", 1)
        weight = from_root(screened[0], "blk", stop_index)
        permuted = jnp.take(current, umklapp_map[stop_index], axis=3)
        d_re, d_im = direct_fold(wavefunc, permuted, weight)
        e_re = e_re + d_re
        e_im = e_im + d_im
    direct = finish_direct(wavefunc, e_re, e_im) * scale_direct
    return lax.psum(direct, "pair") + exchange


def solution(mesh):
    placed = (
        P(("grp", "blk"), None, None, None),
        P(("grp", "blk"), None),
        P(("grp", "blk"), None, None),
        P("grp"),
        P(),
    )
    body = eight_blocks if mesh.shape["blk"] == BLOCKS and mesh.shape["pair"] == 2 else any_blocks
    return jax.shard_map(body, mesh=mesh, in_specs=placed, out_specs=P(("grp", "blk"), None), check_vma=False)
```

```python
import functools
import math

import jax
import jax.numpy as jnp
from jax import lax
from jax.experimental import pallas as pl
from jax.experimental.pallas import tpu as pltpu
from jax.sharding import PartitionSpec as P

NV = 8
NC = 8
STOPS = 2
BF = jnp.bfloat16
F32 = jnp.float32

BLOCKS = 8
OFFSET = {0: 0, 4: 0, 1: 1, 5: 1, 2: 2, 3: 2}
TARGETS = {
    (0, 0): (0, 1), (0, 1): (2, 3),
    (1, 0): (1, 0), (1, 1): (3, 2),
    (2, 0): (2, 0), (2, 1): (6, 4),
    (3, 0): (3, 1), (3, 1): (7, 5),
    (4, 0): (4, 5), (4, 1): (7, 6),
    (5, 0): (5, 4), (5, 1): (6, 7),
}
MATRIX_MOVES = ((0, 4), (1, 5), (2, 3))
FETCH = {
    (0, 0): (3, 2), (0, 1): (1, 2),
    (1, 0): (0, 7), (1, 1): (2, 3),
    (2, 0): (0, None), (2, 1): (6, 4),
    (3, 0): (1, None), (3, 1): (7, 5),
    (4, 0): (5, 6), (4, 1): (7, 6),
    (5, 0): (3, 4), (5, 1): (6, 7),
}
SUMS = ((0, 4), (4, 0))


def pick_cores(pairs, fixed):
    taken, out = {}, []
    for src, dst in pairs:
        chip, core = (src, dst[1]) if fixed == "dst" else (dst, src[1])
        used = taken.setdefault(chip, set())
        core = core if core not in used else 1 - core
        assert core not in used
        used.add(core)
        a, b = ((chip, core), dst) if fixed == "dst" else (src, (chip, core))
        out.append((a[0] * 2 + a[1], b[0] * 2 + b[1]))
    return out


def plan():
    fetch = [pick_cores([(got[r], at) for at, got in FETCH.items() if got[r] is not None], "dst") for r in range(2)]
    home = [
        pick_cores([(at, t[1] if at[1] == 0 else t[0]) for at, t in TARGETS.items()], "src"),
        pick_cores([(at, t[1]) for at, t in TARGETS.items() if at[1] == 1], "src"),
    ]
    table = {}
    for chip, core in TARGETS:
        first, second = FETCH[chip, core]
        held = [chip, first, FETCH[chip, 1 - core][0], second]
        off = OFFSET[chip]
        moved = int(any(d == chip for _, d in MATRIX_MOVES))
        row = [1, off, moved, int(off == 0)]
        row += [held.index(t) for t in TARGETS[chip, core]]
        row += [held.index((t - off) % BLOCKS) for t in TARGETS[chip, core]]
        table[chip, core] = row
    return fetch, home, table


FETCH_ROUNDS, HOME_ROUNDS, TABLE = plan()


def entry(who, column):
    value = jnp.int32(0)
    for b in range(BLOCKS):
        if (b, 0) in TABLE and (TABLE[b, 0][column] or TABLE[b, 1][column]):
            here = jnp.where(who[1] == 0, TABLE[b, 0][column], TABLE[b, 1][column])
            value = jnp.where(who[0] == b, here, value)
    return value


def iota(shape, dim):
    return lax.broadcasted_iota(jnp.int32, shape, dim)


def one(cond, sign=None):
    hit = jnp.where(cond, 1.0, 0.0)
    return hit if sign is None else hit * sign


def dot(a, b, dims=((1,), (0,)), **kw):
    return lax.dot_general(a, b, (dims, ((), ())), preferred_element_type=F32, **kw)


def message_kernel(flat, hay, mine, again):
    rows, planes = flat.shape
    kr = hay.shape[0]
    mine[0:rows, :] = flat[...]
    h = hay[...]
    hi = h.astype(BF)
    lo = (h - hi.astype(F32)).astype(BF)
    both = jnp.concatenate([hi.astype(F32), lo.astype(F32)], axis=1)
    mine[rows : rows + 16, :] = jnp.zeros((16, planes), BF)
    mine[rows : rows + 16, 0:256] = jnp.concatenate([both, jnp.zeros((16 - kr, 256), F32)], axis=0).astype(BF)
    again[0 : rows + 16, :] = mine[...]
    again[rows + 16 :, :] = jnp.zeros((again.shape[0] - rows - 16, planes), BF)


def perm_kernel(who, umk, perm):
    planes = perm.shape[0]
    row = umk[pl.ds(entry(who, 1), 1), :]
    perm[...] = one(iota((planes, planes), 0) == row).astype(BF)


def amplitude(msg, v, c):
    rows = v.shape[0]
    for k in range(rows // 16):
        v[16 * k : 16 * k + 16, :] = msg[32 * k : 32 * k + 16, :]
        c[16 * k : 16 * k + 16, :] = msg[32 * k + 16 : 32 * k + 32, :]
    spread = one(iota((rows, 16), 1) == iota((rows, 16), 0) // 16).astype(BF)
    keep = (iota((rows, 256), 1) % 8) == ((iota((rows, 256), 0) // 2) % 8)
    a = iota((128, rows), 0)
    b = iota((128, rows), 1)
    same_v = ((a // 8) % 8) == ((b // 2) % 8)
    part_a, part_b = a // 64, b % 2
    q0 = one(same_v & (part_a == part_b), jnp.where(part_a == 1, -1.0, 1.0))
    q1 = one(same_v & (part_a != part_b))
    q = jnp.concatenate([q0, q1], axis=1).astype(BF)
    block = (iota((rows, rows), 0) // 16) == (iota((rows, rows), 1) // 16)
    real_row = (iota((rows, rows), 0) % 2) == 0
    x = jnp.where(keep, dot(spread, msg[2 * rows : 2 * rows + 16, 0:256]), 0.0).astype(BF)
    pieces = []
    for piece in (x[:, 0:128], x[:, 128:256]):
        y = dot(piece, q)
        y0, y1 = y[:, :rows], y[:, rows:]
        pieces.append(jnp.where(block, jnp.where(real_row, y0, y1), 0.0).astype(BF))
        pieces.append(jnp.where(block, jnp.where(real_row, y1, -y0), 0.0).astype(BF))
    left = jnp.concatenate([jnp.concatenate(pieces[0::2], axis=1), jnp.concatenate(pieces[1::2], axis=1)], axis=0)
    both = dot(left, jnp.concatenate([v[...], v[...]], axis=0))
    return both[:rows], both[rows:]


def sums(c, amp, turned):
    cf = c[...].astype(F32)
    return jnp.concatenate([jnp.sum(cf * amp, axis=0, keepdims=True), jnp.sum(cf * turned, axis=0, keepdims=True)], axis=0)


def turn_matrix(rows):
    rr, cc = iota((rows, rows), 0), iota((rows, rows), 1)
    pairs = one(rr == (cc + 1 - 2 * (cc % 2)))
    return jnp.where(rr % 2 == 0, pairs, -pairs).astype(BF)


def permute(a, c, perm, ap_refs, wt_refs, cb_refs):
    n = len(ap_refs)
    rows = c.shape[0] // n
    turn = turn_matrix(rows)
    wp = dot(c[...], perm[...])
    ap = dot(a[...], perm[...]).astype(BF)
    for j in range(n):
        part = slice(j * rows, (j + 1) * rows)
        ap_refs[j][0:rows, :] = ap[part]
        ap_refs[j][rows : 2 * rows, :] = dot(turn, ap[part]).astype(BF)
        wt_refs[j][...] = jnp.transpose(wp[part]).astype(BF)
        cb_refs[j][...] = (-dot(turn, c[part, :])).astype(BF)


def prep_kernel(n, n_sums, who, perm, *refs):
    msgs, earlier, (ap, wt, v, ca, cb, xs, a_scr) = refs[:n], refs[n : n + n_sums], refs[n + n_sums :]
    rows, planes = v.shape[1:]
    total = jnp.zeros((2, planes), F32)
    for ref in earlier:
        total = total + ref[...]
    for j in range(n):
        mine = pl.ds(j * rows, rows)
        amp, turned = amplitude(msgs[j], v.at[j], ca.at[mine])
        total = total + sums(ca.at[mine], amp, turned)
        a_scr[mine, :] = amp.astype(BF)
    xs[...] = total

    @pl.when(entry(who, 0) == 1)
    def _():
        each = range(n)
        permute(a_scr, ca, perm, [ap.at[j] for j in each], [wt.at[j] for j in each], [cb.at[j] for j in each])


def pick_kernel(who, perm, msg, earlier, *refs):
    own, two = refs[0:5], refs[5:10]
    ap_ref, wt_ref, vt_ref, ca_ref, cb_ref, xs, ap_3, wt_3, v_3, c_3, cb_3, a_3 = refs[10:]
    rows = v_3.shape[0]

    @pl.when(entry(who, 0) == 1)
    def _():
        amp, turned = amplitude(msg, v_3, c_3)
        a_3[...] = amp.astype(BF)
        xs[...] = earlier[...] + sums(c_3, amp, turned)
        permute(a_3, c_3, perm, [ap_3], [wt_3], [cb_3])

    @pl.when(entry(who, 0) == 0)
    def _():
        xs[...] = jnp.zeros_like(xs)

    def held(slot):
        if slot == 3:
            return ap_3, wt_3, v_3, c_3, cb_3
        ap, wt, v, ca, cb = own if slot == 0 else two
        j = max(slot - 1, 0)
        return ap.at[j], wt.at[j], v.at[j], ca.at[pl.ds(j * rows, rows)], cb.at[j]

    for i in range(2):
        for slot in range(4):

            @pl.when((entry(who, 0) == 1) & (entry(who, 4 + i) == slot))
            def _(i=i, slot=slot):
                _, _, v, ca, cb = held(slot)
                vt_ref[i], ca_ref[i], cb_ref[i] = v[...], ca[...], cb[...]

            @pl.when((entry(who, 0) == 1) & (entry(who, 6 + i) == slot))
            def _(i=i, slot=slot):
                ap, wt = held(slot)[:2]
                ap_ref[i], wt_ref[i] = ap[...], wt[...]


def main_kernel(who, w_own, w_in, w_swapped, ap, wt, v, ca, cb, d_ref, wf):
    rows, planes = v.shape[1:]
    gh = planes // 2
    p = who[1]

    @pl.when((entry(who, 0) == 1) & (entry(who, 2) == 0))
    def _():
        wf[...] = w_own[...]

    @pl.when((entry(who, 0) == 1) & (entry(who, 2) == 1))
    def _():
        wf[pl.ds(pl.multiple_of(p * gh, 128), gh), :] = w_in[...]
        wf[pl.ds(pl.multiple_of((1 - p) * gh, 128), gh), :] = w_swapped[...]

    @pl.when(entry(who, 0) == 1)
    def _():
        kernels = []
        for i in range(2):
            for h in range(2):
                w = wf[h * gh : (h + 1) * gh, :].astype(F32)
                left = wt[i, h * gh : (h + 1) * gh, :]
                k_re = (w * dot(left, ap[i, 0:rows, :])).astype(BF)
                k_im = (w * dot(left, ap[i, rows : 2 * rows, :])).astype(BF)
                kernels.append((k_re, k_im))
        sides = []
        for i in range(2):
            y = None
            for h in range(2):
                k_re, k_im = kernels[2 * i + h]
                part = slice(h * gh, (h + 1) * gh)
                z = dot(ca[i, :, part], k_re) + dot(cb[i, :, part], k_im)
                y = z if y is None else y + z
            sides.append(y.astype(BF))
        for i, y in enumerate(sides):
            d_ref[i] = dot(y, v[i], ((1,), (1,)))


def finish_kernel(scale_direct, scale_exchange, who, d_ref, v, ca, cb, *refs):
    xs, xs_in, coulomb, stays, goes_1, goes_2 = refs
    rows = v.shape[1]
    kr = rows // 16
    p = who[1]
    a = iota((rows, 128), 0)
    b = iota((rows, 128), 1)
    same_v = ((a // 2) % 8) == ((b // 8) % 8)
    ra, rb = a % 2, b // 64
    qa = one(same_v & (ra == rb), jnp.where(rb == 1, -1.0, 1.0))
    qb = one(same_v & (ra != rb))
    q = jnp.concatenate([qa, qb], axis=1).astype(BF)
    real_row = (a % 2) == 0
    keep = (b % 8) == ((a // 2) % 8)
    block = (iota((rows, rows), 0) // 16) == (iota((rows, rows), 1) // 16)

    def result(d):
        d = jnp.where(block, d, 0.0)
        hi = d.astype(BF)
        lo = (d - hi.astype(F32)).astype(BF)
        z = dot(hi, q) + dot(lo, q)
        z = jnp.where(keep, jnp.where(real_row, z[:, :128], z[:, 128:]), 0.0)
        return jnp.sum(z.reshape(kr, 16, 128), axis=1)

    def store(one_, two):
        r1, r2 = result(one_), result(two)
        core_0 = p == 0
        stays[...] = jnp.where(core_0, r1, 0.0)
        goes_1[...] = jnp.where(core_0, r2, r1)
        goes_2[...] = jnp.where(core_0, 0.0, r2)

    @pl.when(entry(who, 0) == 0)
    def _():
        for o in (stays, goes_1, goes_2):
            o[...] = jnp.zeros_like(o)

    @pl.when((entry(who, 0) == 1) & (entry(who, 3) == 0))
    def _():
        store(*(d_ref[i] * scale_direct for i in range(2)))

    @pl.when((entry(who, 0) == 1) & (entry(who, 3) == 1))
    def _():
        y = coulomb[...] * (xs[...] + xs_in[...]) * scale_exchange
        both = []
        for i in range(2):
            side = (ca[i].astype(F32) * y[0:1] + cb[i].astype(F32) * y[1:2]).astype(BF)
            both.append(d_ref[i] * scale_direct + dot(side, v[i], ((1,), (1,))))
        store(*both)


VM = pl.BlockSpec(memory_space=pltpu.VMEM)
SM = pl.BlockSpec(memory_space=pltpu.SMEM)


def call(kernel, outs, ins, scratch=(), known=True, limit=24 << 20):
    moved = sum(math.prod(x.shape) * x.dtype.itemsize for x in (*ins, *outs)) if known else 0
    specs = [SM if x.dtype == jnp.int32 and x.ndim == 1 else VM for x in ins]
    if not known:
        ins = [x if x.dtype == jnp.int32 else pltpu.with_memory_space_constraint(x, pltpu.VMEM) for x in ins]
        outs = [pltpu.VMEM(x.shape, x.dtype) for x in outs]
    return pl.pallas_call(
        kernel,
        out_shape=outs,
        in_specs=specs,
        out_specs=[VM] * len(outs),
        scratch_shapes=list(scratch),
        compiler_params=pltpu.CompilerParams(vmem_limit_bytes=limit),
        cost_estimate=pl.CostEstimate(flops=0, bytes_accessed=moved, transcendentals=0),
    )(*ins)


PAD = 16


def eight_blocks(wavefunc, haydock, screened, coulomb, umklapp_map):
    kr, nb, _, planes = wavefunc.shape
    rows = kr * 16
    gh = planes // 2
    shape = jax.ShapeDtypeStruct
    member = lax.axis_index("pair").astype(jnp.int32)
    who = jnp.stack([lax.axis_index("blk").astype(jnp.int32), member])

    def over_cores(x, pairs):
        return lax.ppermute(x, ("blk", "pair"), pairs)

    def swap(x):
        return lax.ppermute(x, "pair", [(0, 1), (1, 0)])

    def prep(perm, msgs, earlier=(), known=True):
        n = len(msgs)
        outs = [
            shape((n, 2 * rows, planes), BF),
            shape((n, planes, rows), BF),
            shape((n, rows, planes), BF),
            shape((n * rows, planes), BF),
            shape((n, rows, planes), BF),
            shape((2, planes), F32),
        ]
        return call(
            functools.partial(prep_kernel, n, len(earlier)),
            outs,
            [who, perm, *msgs, *earlier],
            scratch=[pltpu.VMEM((n * rows, planes), BF)],
            known=known,
        )

    w_in = lax.ppermute(lax.dynamic_slice_in_dim(screened[0], member * gh, gh, 0), "blk", MATRIX_MOVES)
    flat = wavefunc.reshape(kr * nb * 2, planes)
    sizes = (2 * rows + 16, 2 * rows + 16 + PAD)
    mine, again = call(message_kernel, [shape((n, planes), BF) for n in sizes], [flat, haydock])
    got_1 = over_cores(mine, FETCH_ROUNDS[0])
    (perm,) = call(perm_kernel, [shape((planes, planes), BF)], [who, umklapp_map])
    own = prep(perm, [mine])
    got_1, *own = lax.optimization_barrier((got_1, *own))
    got_2 = over_cores(again, FETCH_ROUNDS[1])
    two = prep(perm, [got_1, swap(got_1)], [own[5]], known=False)
    got_2, *two = lax.optimization_barrier((got_2, *two))
    total_k = kr * lax.axis_size("blk")
    scale_exchange = 1.0 / (8.0 * math.sqrt(planes * total_k))
    scale_direct = -1.0 / (8.0 * math.sqrt(planes * kr * (STOPS + 1)))
    item = shape((2, rows, planes), BF)
    bands = pltpu.VMEM((rows, planes), BF)
    ap, wt, v, ca, cb, xs = call(
        pick_kernel,
        [shape((2, 2 * rows, planes), BF), shape((2, planes, rows), BF), item, item, item, shape((2, planes), F32)],
        [who, perm, got_2, two[5], *own[:5], *two[:5]],
        scratch=[pltpu.VMEM((2 * rows, planes), BF), pltpu.VMEM((planes, rows), BF), bands, bands, bands, bands],
    )
    xs_in = lax.ppermute(xs, "blk", SUMS)
    w_in, ap, wt = lax.optimization_barrier((w_in, ap, wt))
    (d,) = call(
        main_kernel,
        [shape((2, rows, rows), F32)],
        [who, screened[0], w_in, swap(w_in), ap, wt, v, ca, cb],
        scratch=[pltpu.VMEM((planes, planes), BF)],
    )
    stays, goes_1, goes_2 = call(
        functools.partial(finish_kernel, scale_direct, scale_exchange),
        [shape((kr, 128), F32)] * 3,
        [who, d, v, ca, cb, xs, xs_in, coulomb.reshape(1, planes)],
    )
    total = stays + over_cores(goes_1, HOME_ROUNDS[0]) + over_cores(goes_2, HOME_ROUNDS[1])
    return total + swap(total)


def from_root(block, axis, holder):
    block = jnp.where(lax.axis_index(axis) == holder, block, jnp.zeros_like(block))
    return lax.psum(block, axis)


def from_behind(value, axis, by):
    devices = lax.axis_size(axis)
    return lax.ppermute(value, axis, [(i, (i + by) % devices) for i in range(devices)])


def make_amplitude(wave_rows, amp_rows):
    count = wave_rows.shape[0]
    valence = wave_rows[:, :NV].astype(jnp.float32)
    val_re = valence[:, :, 0]
    val_im = valence[:, :, 1]
    amps = amp_rows.reshape(count, 2, NV, NC)
    amp_re = amps[:, 0]
    amp_im = amps[:, 1]
    out_re = jnp.einsum("kvg,kvc->kcg", val_re, amp_re) - jnp.einsum("kvg,kvc->kcg", val_im, amp_im)
    out_im = jnp.einsum("kvg,kvc->kcg", val_re, amp_im) + jnp.einsum("kvg,kvc->kcg", val_im, amp_re)
    return jnp.stack([out_re, out_im], axis=2).astype(jnp.bfloat16)


def densities(wave_rows):
    wide = wave_rows.astype(jnp.float32)
    val_re = wide[:, :NV, 0][:, :, None, :]
    val_im = wide[:, :NV, 1][:, :, None, :]
    cond_re = wide[:, NV:, 0][:, None, :, :]
    cond_im = wide[:, NV:, 1][:, None, :, :]
    return (val_re * cond_re + val_im * cond_im, val_re * cond_im - val_im * cond_re)


def fold_exchange(dens_re, dens_im, amp_rows):
    count = amp_rows.shape[0]
    amps = amp_rows.reshape(count, 2, NV, NC)
    amp_re = amps[:, 0]
    amp_im = amps[:, 1]
    x_re = jnp.einsum("kvcg,kvc->g", dens_re, amp_re) + jnp.einsum("kvcg,kvc->g", dens_im, amp_im)
    x_im = jnp.einsum("kvcg,kvc->g", dens_re, amp_im) - jnp.einsum("kvcg,kvc->g", dens_im, amp_re)
    return (x_re, x_im)


def exchange_terms(dens_re, dens_im, x_re, x_im, coulomb):
    count = dens_re.shape[0]
    y_re = coulomb * x_re
    y_im = coulomb * x_im
    out_re = jnp.einsum("kvcg,g->kvc", dens_re, y_re) - jnp.einsum("kvcg,g->kvc", dens_im, y_im)
    out_im = jnp.einsum("kvcg,g->kvc", dens_re, y_im) + jnp.einsum("kvcg,g->kvc", dens_im, y_re)
    return jnp.stack([out_re, out_im], axis=1).reshape(count, -1)


def direct_fold(wave_rows, permuted, weight):
    valence = wave_rows[:, :NV].astype(jnp.float32)
    val_re = valence[:, :, 0][:, None, :, None, :]
    val_im = valence[:, :, 1][:, None, :, None, :]
    wide = permuted.astype(jnp.float32)
    ahat_re = wide[:, :NC, 0][None, :, None, :, :]
    ahat_im = wide[:, :NC, 1][None, :, None, :, :]
    cond_re = wide[:, NC:, 0]
    cond_im = wide[:, NC:, 1]
    y_re = val_re * ahat_re + val_im * ahat_im
    y_im = val_re * ahat_im - val_im * ahat_re
    stacked = jnp.stack([y_re, y_im], axis=4).astype(jnp.bfloat16)
    flat = stacked.reshape(-1, weight.shape[1])
    image = lax.dot_general(flat, weight, (((1,), (1,)), ((), ())), preferred_element_type=jnp.float32)
    image = image.reshape(stacked.shape)
    z_re = image[:, :, :, :, 0]
    z_im = image[:, :, :, :, 1]
    e_re = jnp.einsum("kjvcg,jcg->kvg", z_re, cond_re) + jnp.einsum("kjvcg,jcg->kvg", z_im, cond_im)
    e_im = jnp.einsum("kjvcg,jcg->kvg", z_im, cond_re) - jnp.einsum("kjvcg,jcg->kvg", z_re, cond_im)
    return (e_re, e_im)


def finish_direct(wave_rows, e_re, e_im):
    count = wave_rows.shape[0]
    cond = wave_rows[:, NV:].astype(jnp.float32)
    cond_re = cond[:, :, 0]
    cond_im = cond[:, :, 1]
    out_re = jnp.einsum("kcg,kvg->kvc", cond_re, e_re) - jnp.einsum("kcg,kvg->kvc", cond_im, e_im)
    out_im = jnp.einsum("kcg,kvg->kvc", cond_re, e_im) + jnp.einsum("kcg,kvg->kvc", cond_im, e_re)
    return jnp.stack([out_re, out_im], axis=1).reshape(count, -1)


def any_blocks(wavefunc, haydock, screened, coulomb, umklapp_map):
    row_count = wavefunc.shape[0]
    plane_count = wavefunc.shape[3]
    share = row_count // lax.axis_size("pair")
    member = lax.axis_index("pair")
    amplitude = make_amplitude(wavefunc, haydock)
    partner = jnp.concatenate([amplitude, wavefunc[:, NV:]], axis=1)
    current = lax.dynamic_slice_in_dim(partner, member * share, share, 0)
    full_re, full_im = densities(wavefunc)
    share_re = lax.dynamic_slice_in_dim(full_re, member * share, share, 0)
    share_im = lax.dynamic_slice_in_dim(full_im, member * share, share, 0)
    hay_share = lax.dynamic_slice_in_dim(haydock, member * share, share, 0)
    x_re, x_im = fold_exchange(share_re, share_im, hay_share)
    x_re, x_im = lax.psum((x_re, x_im), ("blk", "pair"))
    total_k = row_count * lax.axis_size("blk")
    exchange = exchange_terms(full_re, full_im, x_re, x_im, coulomb) * (
        1.0 / (8.0 * math.sqrt(plane_count * total_k))
    )
    scale_direct = -1.0 / (8.0 * math.sqrt(plane_count * row_count * (STOPS + 1)))
    e_re = jnp.zeros((row_count, NV, plane_count), jnp.float32)
    e_im = jnp.zeros((row_count, NV, plane_count), jnp.float32)
    for stop_index in range(STOPS + 1):
        if stop_index > 0:
            current = from_behind(current, "blk", 1)
        weight = from_root(screened[0], "blk", stop_index)
        permuted = jnp.take(current, umklapp_map[stop_index], axis=3)
        d_re, d_im = direct_fold(wavefunc, permuted, weight)
        e_re = e_re + d_re
        e_im = e_im + d_im
    direct = finish_direct(wavefunc, e_re, e_im) * scale_direct
    return lax.psum(direct, "pair") + exchange


def solution(mesh):
    placed = (
        P(("grp", "blk"), None, None, None),
        P(("grp", "blk"), None),
        P(("grp", "blk"), None, None),
        P("grp"),
        P(),
    )
    body = eight_blocks if mesh.shape["blk"] == BLOCKS and mesh.shape["pair"] == 2 else any_blocks
    return jax.shard_map(body, mesh=mesh, in_specs=placed, out_specs=P(("grp", "blk"), None), check_vma=False)
```
